512 devices in a mesh: feat: 32 (over z, core), tok: 16 (over y, x).
Axes of the slice: x: 4, y: 4, z: 16, core: 2. Of those that a mesh axis runs over, the one named last changes fastest.
Arguments:
- enc_rows: bfloat16 [8192, 16384], P('feat', 'tok'), may hold values from -0.75 to 0.75
- dec_rows: bfloat16 [8192, 16384], P('feat', 'tok'), may hold values from -0.046875 to 0.046875
- inputs: bfloat16 [4096, 16384], P('feat', 'tok'), may hold values from -6 to 6
- out_grad: bfloat16 [4096, 16384], P('feat', 'tok'), may hold values from -6 to 6
- destinations: int32 [4096, 2], P('feat'), may hold values from 0 to 31, all different within a row; in each aligned block of 128 rows (0 to 127, 128 to 255, ...) at most 16 rows name the same one
- local_ids: int32 [4096, 2, 32], P('feat'), may hold values from 0 to 255, as said below
- code_values: float32 [4096, 2, 32], P('feat'), may hold values from 0.05 to 2
Outputs:
- enc_grad: bfloat16 [8192, 16384], P('feat', 'tok')
- dec_grad: bfloat16 [8192, 16384], P('feat', 'tok')
- in_grad: bfloat16 [4096, 16384], P('feat', 'tok')
The draws below stay inside these ranges and needn't reach their ends.
Inputs may be any that keep to these rules, and one draw needn't show every extreme that they name: `destinations`: each row names 2 different feat indices; in each aligned block of 128 rows (the tokens of one feat index) no index is named by more than 16 rows, and one index is named by exactly 16 rows. `local_ids`: the 32 numbers of one token and one h are different.
All inputs are finite; a program needn't handle non-finite values.
Results may differ from the reference program's by a relative error of at most 0.0058.
Values may be sent and summed in bfloat16 or wider, within the bound.
No kernel may reach another device: no remote copies, remote signals or barrier semaphores. Data moves between devices by JAX's collectives and lax.ppermute only.
A program may use at most 64 MiB of HBM per device.

```python
import math
import jax
import jax.numpy as jnp
import numpy as np
from jax import lax

D = 16384
F_DEV = 256
K = 64
HOPS = 2
TOK_DEV = 128
PER = 32
CAP = 16
TOKENS = 4096
FEATURES = 8192
N_FEAT = 32


def draw_local_ids(key, part):
    key = jax.random.fold_in(key, 7)
    scores = jax.random.randint(key, (TOKENS, HOPS, F_DEV), 0, 1 << 20)
    scores = scores * F_DEV + jnp.arange(F_DEV, dtype=jnp.int32)
    _, picked = lax.top_k(scores, PER)
    return picked.astype(jnp.int32)


def levels(stream_key, shape, cuts, least, top_value):
    gain, own = 1.0, jax.random.fold_in(stream_key, 6)
    for dim, shards_of in cuts:
        steps = jnp.exp(jax.random.uniform(jax.random.fold_in(own, dim), (shards_of,), jnp.float32, least / len(cuts), top_value / len(cuts)))
        gain = gain * jnp.repeat(steps, shape[dim] // shards_of).reshape([-1 if axis == dim else 1 for axis in range(len(shape))])
    return gain


def routed_block(stream_key, own, number, rows, amount, top, most, skew):
    ranking = jax.random.permutation(stream_key, amount)
    packed, common = shares(amount, rows * top, most, skew, True), shares(amount, rows * top, most, skew, False)
    places = jnp.arange(amount)

    def named(tallies, rotation):
        used = int((tallies > 0).sum())
        fixed = max(1, used // 4)
        passed = fixed + (places - fixed + rotation * (used - fixed)) % max(1, amount - fixed)
        return jnp.zeros((amount,), jnp.int32).at[ranking[jnp.where(places < fixed, places, passed)]].set(jnp.asarray(tallies, jnp.int32))

    tallies = jnp.where(number % 4 == 0, named(packed, number // 4), named(common, number - number // 4 - 1))
    mixed = jax.random.permutation(jax.random.fold_in(own, 3), amount)
    donor, receiver = mixed[0:amount // 2 * 2:2], mixed[1:amount // 2 * 2:2]
    room = jnp.minimum(tallies[donor] - 1, most - tallies[receiver]) // 2
    room = jnp.where((donor == ranking[0]) | (receiver == ranking[0]) | (tallies[receiver] == 0), 0, jnp.maximum(room, 0))
    passed = jax.random.randint(jax.random.fold_in(own, 4), (amount // 2,), 0, 1 << 20) % (room + 1)
    tallies = tallies.at[donor].add(-passed).at[receiver].add(passed)
    labels = jnp.searchsorted(jnp.cumsum(tallies), jnp.arange(rows * top), side="right").astype(jnp.int32)
    table = labels.reshape(top, rows).T
    table = table[jax.random.permutation(jax.random.fold_in(own, 1), rows)]
    rotation = jax.random.randint(jax.random.fold_in(own, 2), (rows, 1), 0, top)
    return jnp.take_along_axis(table, (jnp.arange(top)[None, :] + rotation) % top, axis=1)


def shares(count, total, reach, lean, full):
    weights = [(1 << 20) // math.isqrt(standing ** lean) + 1 for standing in range(1, count + 1)]
    largest = reach if full else min(reach, max(-(-total // count), total * weights[0] // sum(weights)))
    least = 1 if total - largest >= count - 1 else 0
    given, rest = [largest] + [least] * (count - 1), total - largest - least * (count - 1)
    while rest > 0:
        movable = [i for i in range(1, count) if given[i] < largest] or [i for i in range(1, count) if given[i] < reach]
        pool, remaining = sum([weights[i] for i in movable]), rest
        for i in movable:
            addition = min(reach - given[i], max(1, remaining * weights[i] // pool), rest)
            given[i] = given[i] + addition
            rest = rest - addition
    return np.array(given)


def scatter_about(own_key, shape, spread, limit, shards=(), kind=jnp.bfloat16):
    values = jax.random.normal(own_key, shape, jnp.float32) * spread
    if len(shards) > 0:
        values = levels(own_key, shape, shards, -0.22, 0.18) * values
    return jnp.clip(values, min=-limit, max=limit).astype(kind)


def setup_inputs(seed: int = 0) -> dict:
    arg_keys = jax.random.split(jax.random.key(seed), 8)
    enc_rows = scatter_about(arg_keys[0], (FEATURES, D), K ** -0.5, 0.75, ((0, 32), (1, 16)))
    dec_rows = scatter_about(arg_keys[1], (FEATURES, D), D ** -0.5, 0.046875, ((0, 32), (1, 16)))
    inputs = scatter_about(arg_keys[2], (TOKENS, D), 1.0, 6.0, ((0, 32), (1, 16)))
    out_grad = scatter_about(arg_keys[3], (TOKENS, D), 1.0, 6.0, ((0, 32), (1, 16)))
    destinations_keys = jax.random.split(jax.random.fold_in(arg_keys[4], 1), TOKENS // TOK_DEV)
    destinations_turns = jax.random.permutation(jax.random.fold_in(arg_keys[4], 3), TOKENS // TOK_DEV)
    destinations = jax.vmap(lambda own, number: routed_block(jax.random.fold_in(arg_keys[4], 2), own, number, TOK_DEV, N_FEAT, HOPS, CAP, 2))(destinations_keys, destinations_turns).reshape((TOKENS, HOPS))
    local_ids = draw_local_ids(jax.random.fold_in(arg_keys[7], 71), 0)
    code_values = jnp.clip(jnp.exp(math.log(2.0) - 3.6888794 * jax.random.uniform(arg_keys[6], (TOKENS, HOPS, PER), jnp.float32) ** levels(arg_keys[6], (TOKENS, HOPS, PER), ((0, 32),), -0.2, 0.2)), 0.05, 2.0)
    return dict(enc_rows=enc_rows, dec_rows=dec_rows, inputs=inputs, out_grad=out_grad, destinations=destinations, local_ids=local_ids, code_values=code_values)


def reference(enc_rows, dec_rows, inputs, out_grad, destinations, local_ids, code_values):
    pair_count = TOKENS * HOPS
    group_size = 32
    block_count = pair_count // group_size
    slot_total = N_FEAT * CAP
    flat_dest = destinations.reshape(pair_count).astype(jnp.int32)
    pair_token = (jnp.arange(pair_count, dtype=jnp.int32) // HOPS).astype(jnp.int32)
    pair_ids = local_ids.reshape(pair_count, PER).astype(jnp.int32)
    pair_codes = code_values.reshape(pair_count, PER).astype(jnp.bfloat16)
    feature_of = (flat_dest[:, None] * F_DEV + pair_ids).astype(jnp.int32)

    def pair_block(block_args):
        feature_block, token_block = block_args
        grad_rows = jnp.take(out_grad, token_block, axis=0).astype(jnp.float32)
        dec_pick = jnp.take(dec_rows, feature_block, axis=0).astype(jnp.float32)
        code_grad = jnp.einsum("gpd,gd->gp", dec_pick, grad_rows)
        pre_grad = code_grad.astype(jnp.bfloat16)
        enc_pick = jnp.take(enc_rows, feature_block, axis=0).astype(jnp.float32)
        hop_term = jnp.einsum("gpd,gp->gd", enc_pick, pre_grad.astype(jnp.float32)).astype(jnp.bfloat16)
        return pre_grad, hop_term

    pre_grad, hop_term = lax.map(
        pair_block,
        (feature_of.reshape(block_count, group_size, PER), pair_token.reshape(block_count, group_size)),
    )
    pre_grad = pre_grad.reshape(pair_count, PER)
    hop_term = lax.optimization_barrier(hop_term.reshape(TOKENS, HOPS, D))
    in_grad = jnp.sum(hop_term.astype(jnp.float32), axis=1).astype(jnp.bfloat16)

    def device_grads(device):
        matches = (flat_dest == device).astype(jnp.int32)
        position = jnp.cumsum(matches) - matches
        slot_spot = jnp.where(matches > 0, position, slot_total).astype(jnp.int32)
        slot_table = jnp.full((slot_total,), pair_count, jnp.int32).at[slot_spot].set(
            jnp.arange(pair_count, dtype=jnp.int32), mode="drop")
        slot_ids = jnp.take(pair_ids, slot_table, axis=0, mode="fill", fill_value=0).astype(jnp.int32)
        slot_codes = jnp.take(pair_codes, slot_table, axis=0, mode="fill", fill_value=0)
        slot_pre = jnp.take(pre_grad, slot_table, axis=0, mode="fill", fill_value=0)
        slot_tokens = jnp.take(pair_token, slot_table, axis=0, mode="fill", fill_value=0).astype(jnp.int32)
        grad_rows = jnp.take(out_grad, slot_tokens, axis=0)
        input_rows = jnp.take(inputs, slot_tokens, axis=0)
        slot_order = jnp.arange(slot_total, dtype=jnp.int32)[:, None]
        code_mat = jnp.zeros((slot_total, F_DEV), jnp.bfloat16).at[slot_order, slot_ids].set(slot_codes)
        pre_mat = jnp.zeros((slot_total, F_DEV), jnp.bfloat16).at[slot_order, slot_ids].set(slot_pre)
        dec_part = jnp.dot(code_mat.T, grad_rows, preferred_element_type=jnp.float32).astype(jnp.bfloat16)
        enc_part = jnp.dot(pre_mat.T, input_rows, preferred_element_type=jnp.float32).astype(jnp.bfloat16)
        return enc_part, dec_part

    enc_all, dec_all = lax.map(device_grads, jnp.arange(N_FEAT, dtype=jnp.int32))
    enc_grad = enc_all.reshape(FEATURES, D)
    dec_grad = dec_all.reshape(FEATURES, D)
    return enc_grad, dec_grad, in_grad
```

```python
import functools

import jax
import jax.numpy as jnp
from jax import lax
from jax.experimental import pallas as pl
from jax.experimental.pallas import tpu as pltpu
from jax.sharding import PartitionSpec as P

F32 = jnp.float32
BF16 = jnp.bfloat16
LANES = 128
VMEM_BYTES = 48 * 1024 * 1024
ROWS_ROWS = (((1,), (1,)), ((), ()))
DEPTH_FIRST = (((0,), (0,)), ((), ()))


def call(kernel, outs, flops, moved):
    return pl.pallas_call(
        kernel,
        out_shape=outs,
        compiler_params=pltpu.CompilerParams(vmem_limit_bytes=VMEM_BYTES),
        cost_estimate=pl.CostEstimate(flops=flops, bytes_accessed=moved, transcendentals=0),
    )


def pick_matrices(dest_ref, groups, capacity, slot_count):
    tokens = dest_ref.shape[1]
    group_line = lax.broadcasted_iota(jnp.int32, (groups, tokens), 0)
    earlier = (
        lax.broadcasted_iota(jnp.int32, (tokens, tokens), 0)
        < lax.broadcasted_iota(jnp.int32, (tokens, tokens), 1)
    ).astype(F32).astype(BF16)
    slot_line = lax.broadcasted_iota(jnp.int32, (slot_count, tokens), 0)
    taken = jnp.zeros((groups, 1), F32)
    out = []
    for hop in range(dest_ref.shape[0]):
        dest = dest_ref[hop : hop + 1, :]
        match = (group_line == dest).astype(F32)
        before = jnp.dot(match.astype(BF16), earlier, preferred_element_type=F32) + taken
        place = jnp.sum(before * match, axis=0, keepdims=True).astype(jnp.int32)
        out.append((slot_line == dest * capacity + place).astype(F32).astype(BF16))
        taken = taken + jnp.sum(match, axis=1, keepdims=True)
    return out


def pack_kernel(groups, capacity, dest_ref, ids_ref, codes_ref, grads_ref, inputs_ref, row_ref, input_ref):
    slot_count, width = input_ref.shape
    tokens = grads_ref.shape[0]
    picks = pick_matrices(dest_ref, groups, capacity, slot_count)
    pick = functools.reduce(jnp.add, picks)
    row_ref[:, :width] = jnp.dot(pick, grads_ref[...], preferred_element_type=F32).astype(BF16)
    per = ids_ref.shape[1]
    notes = jnp.zeros((slot_count, LANES), F32)
    for hop, hop_pick in enumerate(picks):
        lines = jnp.concatenate(
            [
                ids_ref[hop].astype(F32),
                codes_ref[hop],
                jnp.zeros((LANES - 2 * per, tokens), F32),
            ],
            axis=0,
        ).astype(BF16)
        notes = notes + lax.dot_general(hop_pick, lines, ROWS_ROWS, preferred_element_type=F32)
    row_ref[:, width:] = notes.astype(BF16)
    input_ref[...] = jnp.dot(pick, inputs_ref[...], preferred_element_type=F32).astype(BF16)


def fold(values, per):
    parts = LANES // per
    height = values.shape[0] // parts
    lane = lax.broadcasted_iota(jnp.int32, (height, LANES), 1)
    out = values[:height]
    for q in range(1, parts):
        turned = pltpu.roll(values[q * height : (q + 1) * height], q * per, 1)
        out = jnp.where(lane >= q * per, turned, out)
    return out


def score_kernel(per, row_ref, dec_ref, score_ref, ids_ref, codes_ref):
    width = dec_ref.shape[1]
    scores = lax.dot_general(row_ref[:, :width], dec_ref[...], ROWS_ROWS, preferred_element_type=F32)
    notes = row_ref[:, width:].astype(F32)
    ids = notes.astype(jnp.int32)
    low = ids & (LANES - 1)
    chosen = jnp.take_along_axis(scores[:, :LANES], low, axis=1)
    for part in range(1, dec_ref.shape[0] // LANES):
        here = jnp.take_along_axis(scores[:, part * LANES : (part + 1) * LANES], low, axis=1)
        chosen = jnp.where(ids >= part * LANES, here, chosen)
    folded = fold(chosen, per)
    for copy in range(score_ref.shape[0]):
        score_ref[copy] = folded
    ids_ref[...] = fold(notes, per).T
    codes_ref[...] = fold(pltpu.roll(notes, LANES - per, 1), per).T


def spread(ids, values, features, per):
    held = ids.shape[1]
    feature_line = lax.broadcasted_iota(jnp.int32, (features, held), 0).astype(F32)
    blocks = []
    for q in range(LANES // per):
        block = jnp.zeros((features, held), F32)
        for j in range(q * per, (q + 1) * per):
            block = jnp.where(feature_line == ids[j : j + 1, :], values[j : j + 1, :], block)
        blocks.append(block)
    return jnp.concatenate(blocks, axis=1).astype(BF16)


def back_kernel(per, score_ref, ids_ref, enc_ref, pre_ref, back_ref):
    total = score_ref[0]
    for copy in range(1, score_ref.shape[0]):
        total = total + score_ref[copy]
    rounded = total.astype(BF16).astype(F32).T
    pre = spread(ids_ref[...], rounded, enc_ref.shape[0], per)
    pre_ref[...] = pre
    back_ref[...] = lax.dot_general(pre, enc_ref[...], DEPTH_FIRST, preferred_element_type=F32).astype(BF16)


def dec_kernel(per, ids_ref, codes_ref, row_ref, out_ref):
    features, width = out_ref.shape
    code = spread(ids_ref[...], codes_ref[...], features, per)
    out_ref[...] = jnp.dot(code, row_ref[:, :width], preferred_element_type=F32).astype(BF16)


def enc_kernel(pre_ref, input_ref, out_ref):
    out_ref[...] = jnp.dot(pre_ref[...], input_ref[...], preferred_element_type=F32).astype(BF16)


def merge_kernel(groups, capacity, dest_ref, back_ref, out_ref):
    picks = pick_matrices(dest_ref, groups, capacity, back_ref.shape[0])
    pick = functools.reduce(jnp.add, picks)
    out_ref[...] = lax.dot_general(pick, back_ref[...], DEPTH_FIRST, preferred_element_type=F32).astype(BF16)


def shards(enc_rows, dec_rows, inputs, out_grad, destinations, local_ids, code_values):
    groups = lax.axis_size("feat")
    slices = lax.axis_size("tok")
    tokens, hops = destinations.shape
    per = local_ids.shape[2]
    features, width = dec_rows.shape
    capacity = max(2, 2 * tokens * hops // groups)
    slots = groups * capacity
    dest = destinations.T
    shape = jax.ShapeDtypeStruct
    mac = 2 * slots * width

    send_rows, send_inputs = call(
        functools.partial(pack_kernel, groups, capacity),
        (shape((slots, width + LANES), BF16), shape((slots, width), BF16)),
        2 * mac * tokens,
        4 * slots * width + 4 * tokens * width,
    )(dest, jnp.transpose(local_ids, (1, 2, 0)), jnp.transpose(code_values, (1, 2, 0)), out_grad, inputs)

    rows = lax.all_to_all(
        send_rows.reshape(groups, capacity, width + LANES), "feat", split_axis=0, concat_axis=0, tiled=True
    ).reshape(slots, width + LANES)
    held = slots * per // LANES
    score, ids, codes = call(
        functools.partial(score_kernel, per),
        (shape((slices, held, LANES), F32), shape((LANES, held), F32), shape((LANES, held), F32)),
        mac * features,
        2 * slots * width,
    )(rows, dec_rows)
    score = lax.all_to_all(score, "tok", split_axis=0, concat_axis=0, tiled=True)
    pre, back = call(
        functools.partial(back_kernel, per),
        (shape((features, slots), BF16), shape((slots, width), BF16)),
        mac * features,
        2 * slots * width,
    )(score, ids, enc_rows)
    returned = lax.all_to_all(
        back.reshape(groups, capacity, width), "feat", split_axis=0, concat_axis=0, tiled=True
    ).reshape(slots, width)
    dec_grad = call(
        functools.partial(dec_kernel, per), shape((features, width), BF16), mac * features, 4 * slots * width
    )(ids, codes, rows)
    given = lax.all_to_all(
        send_inputs.reshape(groups, capacity, width), "feat", split_axis=0, concat_axis=0, tiled=True
    ).reshape(slots, width)
    enc_grad = call(enc_kernel, shape((features, width), BF16), mac * features, 4 * slots * width)(pre, given)
    in_grad = call(
        functools.partial(merge_kernel, groups, capacity),
        shape((tokens, width), BF16),
        mac * tokens,
        4 * slots * width,
    )(dest, returned)
    return (enc_grad, dec_grad, in_grad)


def solution(mesh):
    split = P("feat", "tok")
    return jax.shard_map(
        shards,
        mesh=mesh,
        in_specs=(split, split, split, split, P("feat", None), P("feat", None, None), P("feat", None, None)),
        out_specs=(split, split, split),
        check_vma=False,
    )
```

```python
import functools

import jax
import jax.numpy as jnp
from jax import lax
from jax.experimental import pallas as pl
from jax.experimental.pallas import tpu as pltpu
from jax.sharding import PartitionSpec as P

F32 = jnp.float32
BF16 = jnp.bfloat16
LANES = 128
EARLY = (8, 7)
VMEM_BYTES = 48 * 1024 * 1024
ROWS_ROWS = (((1,), (1,)), ((), ()))
DEPTH_FIRST = (((0,), (0,)), ((), ()))


def call(kernel, outs, flops, moved, scratch=(), plain=0, order_only=0):
    specs = {}
    if order_only:
        specs["in_specs"] = [pl.BlockSpec(memory_space=pltpu.VMEM)] * plain
        specs["in_specs"] += [pl.BlockSpec(memory_space=pl.ANY)] * order_only
    return pl.pallas_call(
        kernel,
        **specs,
        out_shape=outs,
        scratch_shapes=scratch,
        compiler_params=pltpu.CompilerParams(vmem_limit_bytes=VMEM_BYTES),
        cost_estimate=pl.CostEstimate(flops=flops, bytes_accessed=moved, transcendentals=0),
    )


def places(dest_ref, groups):
    tokens = dest_ref.shape[1]
    group_line = lax.broadcasted_iota(jnp.int32, (groups, tokens), 0)
    earlier = (
        lax.broadcasted_iota(jnp.int32, (tokens, tokens), 0)
        < lax.broadcasted_iota(jnp.int32, (tokens, tokens), 1)
    ).astype(F32).astype(BF16)
    taken = jnp.zeros((groups, 1), F32)
    out = []
    for hop in range(dest_ref.shape[0]):
        match = (group_line == dest_ref[hop : hop + 1, :]).astype(F32)
        before = jnp.dot(match.astype(BF16), earlier, preferred_element_type=F32) + taken
        out.append(jnp.sum(before * match, axis=0, keepdims=True).astype(jnp.int32))
        taken = taken + jnp.sum(match, axis=1, keepdims=True)
    return out


def one_hot(numbers, count):
    line = lax.broadcasted_iota(jnp.int32, (count, numbers.shape[1]), 0)
    return (line == numbers).astype(F32).astype(BF16)


def pick_matrices(dest_ref, groups, capacity):
    return [
        one_hot(dest_ref[hop : hop + 1, :] * capacity + place, groups * capacity)
        for hop, place in enumerate(places(dest_ref, groups))
    ]


def relative_slots(dest, place, groups, capacity):
    me = lax.axis_index("feat")
    chips = groups // 2
    core = me & 1
    away = ((dest >> 1) - (me >> 1)) & (chips - 1)
    away = jnp.where(core == 1, (chips - away) & (chips - 1), away)
    far = capacity + (away - 1) * 2 * capacity + (dest & 1) * capacity
    here = jnp.where((dest & 1) == core, 0, (groups - 1) * capacity)
    return jnp.where(away == 0, here, far) + place


def pack_rows_kernel(groups, capacity, dest_ref, ids_ref, codes_ref, grads_ref, row_ref):
    slot_count = row_ref.shape[0]
    tokens, width = grads_ref.shape
    picks = pick_matrices(dest_ref, groups, capacity)
    pick = functools.reduce(jnp.add, picks)
    row_ref[:, :width] = jnp.dot(pick, grads_ref[...], preferred_element_type=F32).astype(BF16)
    per = ids_ref.shape[1]
    notes = jnp.zeros((slot_count, LANES), F32)
    for hop, hop_pick in enumerate(picks):
        lines = jnp.concatenate(
            [
                ids_ref[hop].astype(F32),
                codes_ref[hop],
                jnp.zeros((LANES - 2 * per, tokens), F32),
            ],
            axis=0,
        ).astype(BF16)
        notes = notes + lax.dot_general(hop_pick, lines, ROWS_ROWS, preferred_element_type=F32)
    row_ref[:, width:] = notes.astype(BF16)


def pack_inputs_kernel(groups, capacity, dest_ref, inputs_ref, keep_ref, give_ref):
    kept = keep_ref.shape[0]
    numbers = [
        relative_slots(dest_ref[hop : hop + 1, :], place, groups, capacity)
        for hop, place in enumerate(places(dest_ref, groups))
    ]
    pick = functools.reduce(jnp.add, [one_hot(number, groups * capacity) for number in numbers])
    chosen = jnp.dot(pick, inputs_ref[...], preferred_element_type=F32).astype(BF16)
    keep_ref[...] = chosen[:kept]
    give_ref[...] = chosen[kept:]


def join_kernel(capacity, reach, picked, keep_ref, got_ref, after_ref, *out_refs):
    del after_ref
    for k, out_ref in zip(picked, out_refs, strict=True):
        if k > reach:
            mine = capacity + reach * 2 * capacity
            out_ref[...] = keep_ref[mine : mine + 2 * capacity, :]
            continue
        for core in range(2):
            mine = capacity + ((k - 1) * 2 + core) * capacity
            theirs = ((reach - k) * 2 + core) * capacity
            out_ref[2 * core * capacity : (2 * core + 1) * capacity, :] = keep_ref[mine : mine + capacity, :]
            out_ref[(2 * core + 1) * capacity : (2 * core + 2) * capacity, :] = got_ref[theirs : theirs + capacity, :]


def cross_kernel(capacity, far_ref, *refs):
    message_refs, out_ref = refs[:-1], refs[-1]
    other = 1 - (lax.axis_index("feat") & 1)
    for k, ref in enumerate(message_refs):
        start = pl.multiple_of(other * 2 * capacity, 2 * capacity)
        out_ref[k * 2 * capacity : (k + 1) * 2 * capacity, :] = ref[pl.ds(start, 2 * capacity), :]
    start = pl.multiple_of(other * capacity, capacity)
    out_ref[len(message_refs) * 2 * capacity :, :] = far_ref[pl.ds(start, capacity), :]


def enc_kernel(groups, capacity, pre_ref, keep_ref, got_ref, far_ref, crossed_ref, *refs):
    message_refs, out_ref, line_ref = refs[:-2], refs[-2], refs[-1]
    me = lax.axis_index("feat")
    chips = groups // 2
    chip, core = me >> 1, me & 1
    other = 1 - core
    reach = len(message_refs)

    def put(away, owner, rows):
        source = ((chip + away) & (chips - 1)) * 2 + owner
        line_ref[pl.ds(pl.multiple_of(source * capacity, capacity), capacity), :] = rows

    put(0, core, keep_ref[:capacity, :])
    put(0, other, got_ref[got_ref.shape[0] - capacity :, :])
    put(chips // 2, core, far_ref[pl.ds(pl.multiple_of(core * capacity, capacity), capacity), :])
    put(chips // 2, other, crossed_ref[reach * 2 * capacity :, :])
    for k in range(1, reach + 1):
        away = jnp.where(core == 0, chips - k, k)
        base = pl.multiple_of(core * 2 * capacity, 2 * capacity)
        put(away, core, message_refs[k - 1][pl.ds(base, capacity), :])
        put(away, other, message_refs[k - 1][pl.ds(base + capacity, capacity), :])
        base = (k - 1) * 2 * capacity
        put(chips - away, other, crossed_ref[base : base + capacity, :])
        put(chips - away, core, crossed_ref[base + capacity : base + 2 * capacity, :])
    out_ref[...] = jnp.dot(pre_ref[...], line_ref[...], preferred_element_type=F32).astype(BF16)


def fold(values, per):
    parts = LANES // per
    height = values.shape[0] // parts
    lane = lax.broadcasted_iota(jnp.int32, (height, LANES), 1)
    out = values[:height]
    for q in range(1, parts):
        turned = pltpu.roll(values[q * height : (q + 1) * height], q * per, 1)
        out = jnp.where(lane >= q * per, turned, out)
    return out


def score_kernel(per, row_ref, dec_ref, score_ref, ids_ref, codes_ref):
    width = dec_ref.shape[1]
    scores = lax.dot_general(row_ref[:, :width], dec_ref[...], ROWS_ROWS, preferred_element_type=F32)
    notes = row_ref[:, width:].astype(F32)
    ids = notes.astype(jnp.int32)
    low = ids & (LANES - 1)
    chosen = jnp.take_along_axis(scores[:, :LANES], low, axis=1)
    for part in range(1, dec_ref.shape[0] // LANES):
        here = jnp.take_along_axis(scores[:, part * LANES : (part + 1) * LANES], low, axis=1)
        chosen = jnp.where(ids >= part * LANES, here, chosen)
    folded = fold(chosen, per)
    for copy in range(score_ref.shape[0]):
        score_ref[copy] = folded
    ids_ref[...] = fold(notes, per).T
    codes_ref[...] = fold(pltpu.roll(notes, LANES - per, 1), per).T


def spread(ids, values, features, per):
    held = ids.shape[1]
    feature_line = lax.broadcasted_iota(jnp.int32, (features, held), 0).astype(F32)
    blocks = []
    for q in range(LANES // per):
        block = jnp.zeros((features, held), F32)
        for j in range(q * per, (q + 1) * per):
            block = jnp.where(feature_line == ids[j : j + 1, :], values[j : j + 1, :], block)
        blocks.append(block)
    return jnp.concatenate(blocks, axis=1).astype(BF16)


def back_kernel(per, score_ref, ids_ref, enc_ref, *refs):
    pre_ref, back_ref = refs[-2:]
    total = score_ref[0]
    for copy in range(1, score_ref.shape[0]):
        total = total + score_ref[copy]
    rounded = total.astype(BF16).astype(F32).T
    pre = spread(ids_ref[...], rounded, enc_ref.shape[0], per)
    pre_ref[...] = pre
    back_ref[...] = lax.dot_general(pre, enc_ref[...], DEPTH_FIRST, preferred_element_type=F32).astype(BF16)


def dec_kernel(per, ids_ref, codes_ref, row_ref, out_ref):
    features, width = out_ref.shape
    code = spread(ids_ref[...], codes_ref[...], features, per)
    out_ref[...] = jnp.dot(code, row_ref[:, :width], preferred_element_type=F32).astype(BF16)


def merge_kernel(groups, capacity, dest_ref, back_ref, out_ref):
    picks = pick_matrices(dest_ref, groups, capacity)
    pick = functools.reduce(jnp.add, picks)
    out_ref[...] = lax.dot_general(pick, back_ref[...], DEPTH_FIRST, preferred_element_type=F32).astype(BF16)


def shards(enc_rows, dec_rows, inputs, out_grad, destinations, local_ids, code_values):
    groups = lax.axis_size("feat")
    slices = lax.axis_size("tok")
    tokens, hops = destinations.shape
    per = local_ids.shape[2]
    features, width = dec_rows.shape
    capacity = max(2, 2 * tokens * hops // groups)
    slots = groups * capacity
    dest = destinations.T
    shape = jax.ShapeDtypeStruct
    mac = 2 * slots * width

    send_rows = call(
        functools.partial(pack_rows_kernel, groups, capacity),
        shape((slots, width + LANES), BF16),
        mac * tokens,
        2 * slots * width + 2 * tokens * width,
    )(dest, jnp.transpose(local_ids, (1, 2, 0)), jnp.transpose(code_values, (1, 2, 0)), out_grad)
    rows = lax.all_to_all(
        send_rows.reshape(groups, capacity, width + LANES), "feat", split_axis=0, concat_axis=0, tiled=True
    ).reshape(slots, width + LANES)

    chips = groups // 2
    reach = chips // 2 - 1
    given = (reach * 2 + 1) * capacity
    keep, give = call(
        functools.partial(pack_inputs_kernel, groups, capacity),
        (shape((slots - given, width), BF16), shape((given, width), BF16)),
        mac * tokens,
        2 * slots * width + 2 * tokens * width,
    )(dest, inputs)
    swap = [(i, i ^ 1) for i in range(groups)]
    got = lax.ppermute(give, "feat", swap)

    def away(k):
        return [(i, ((i // 2 + (chips - k if i % 2 else k)) % chips) * 2 + i % 2) for i in range(groups)]

    def send(picked, after):
        messages = call(
            functools.partial(join_kernel, capacity, reach, picked),
            tuple(shape(((4 if k <= reach else 2) * capacity, width), BF16) for k in picked),
            0,
            4 * len(picked) * 4 * capacity * width,
            plain=2,
            order_only=1,
        )(keep, got, after)
        return {k: lax.ppermute(m, "feat", away(k)) for k, m in zip(picked, messages, strict=True)}

    arrived = send(EARLY, rows)
    held = slots * per // LANES
    score, ids, codes = call(
        functools.partial(score_kernel, per),
        (shape((slices, held, LANES), F32), shape((LANES, held), F32), shape((LANES, held), F32)),
        mac * features,
        2 * slots * width,
    )(rows, dec_rows)
    score = lax.all_to_all(score, "tok", split_axis=0, concat_axis=0, tiled=True)
    pre, back = call(
        functools.partial(back_kernel, per),
        (shape((features, slots), BF16), shape((slots, width), BF16)),
        mac * features,
        2 * slots * width,
        plain=3,
        order_only=len(EARLY),
    )(score, ids, enc_rows, *[arrived[k] for k in EARLY])
    returned = lax.all_to_all(
        back.reshape(groups, capacity, width), "feat", split_axis=0, concat_axis=0, tiled=True
    ).reshape(slots, width)
    arrived |= send(tuple(k for k in range(reach, 0, -1) if k not in EARLY), back)
    far = arrived[reach + 1]
    arrived = [arrived[k] for k in range(1, reach + 1)]
    crossed = lax.ppermute(
        call(functools.partial(cross_kernel, capacity), shape((given, width), BF16), 0, 4 * given * width)(
            far, *arrived
        ),
        "feat",
        swap,
    )
    dec_grad = call(
        functools.partial(dec_kernel, per), shape((features, width), BF16), mac * features, 4 * slots * width
    )(ids, codes, rows)
    enc_grad = call(
        functools.partial(enc_kernel, groups, capacity),
        shape((features, width), BF16),
        mac * features,
        4 * slots * width,
        (pltpu.VMEM((slots, width), BF16),),
    )(pre, keep, got, far, crossed, *arrived)
    in_grad = call(
        functools.partial(merge_kernel, groups, capacity),
        shape((tokens, width), BF16),
        mac * tokens,
        4 * slots * width,
    )(dest, returned)
    return (enc_grad, dec_grad, in_grad)


def solution(mesh):
    split = P("feat", "tok")
    return jax.shard_map(
        shards,
        mesh=mesh,
        in_specs=(split, split, split, split, P("feat", None), P("feat", None, None), P("feat", None, None)),
        out_specs=(split, split, split),
        check_vma=False,
    )
```

```python
import functools

import jax
import jax.numpy as jnp
from jax import lax
from jax.experimental import pallas as pl
from jax.experimental.pallas import tpu as pltpu
from jax.sharding import PartitionSpec as P

F32 = jnp.float32
BF16 = jnp.bfloat16
LANES = 128
DEVICES_A_STEP = 4
VMEM_BYTES = 48 * 1024 * 1024
ROWS_ROWS = (((1,), (1,)), ((), ()))
DEPTH_FIRST = (((0,), (0,)), ((), ()))


def call(kernel, outs, flops, moved, **how):
    return pl.pallas_call(
        kernel,
        out_shape=outs,
        **how,
        compiler_params=pltpu.CompilerParams(vmem_limit_bytes=VMEM_BYTES),
        cost_estimate=pl.CostEstimate(flops=flops, bytes_accessed=moved, transcendentals=0),
    )


def pick_matrices(dest_ref, groups, capacity, slot_count):
    tokens = dest_ref.shape[1]
    group_line = lax.broadcasted_iota(jnp.int32, (groups, tokens), 0)
    earlier = (
        lax.broadcasted_iota(jnp.int32, (tokens, tokens), 0)
        < lax.broadcasted_iota(jnp.int32, (tokens, tokens), 1)
    ).astype(F32).astype(BF16)
    slot_line = lax.broadcasted_iota(jnp.int32, (slot_count, tokens), 0)
    taken = jnp.zeros((groups, 1), F32)
    out = []
    for hop in range(dest_ref.shape[0]):
        dest = dest_ref[hop : hop + 1, :]
        match = (group_line == dest).astype(F32)
        before = jnp.dot(match.astype(BF16), earlier, preferred_element_type=F32) + taken
        place = jnp.sum(before * match, axis=0, keepdims=True).astype(jnp.int32)
        out.append((slot_line == dest * capacity + place).astype(F32).astype(BF16))
        taken = taken + jnp.sum(match, axis=1, keepdims=True)
    return out


def pack_kernel(groups, capacity, dest_ref, ids_ref, codes_ref, grads_ref, row_ref):
    slot_count = row_ref.shape[0]
    tokens, width = grads_ref.shape
    picks = pick_matrices(dest_ref, groups, capacity, slot_count)
    pick = functools.reduce(jnp.add, picks)
    row_ref[:, :width] = jnp.dot(pick, grads_ref[...], preferred_element_type=F32).astype(BF16)
    per = ids_ref.shape[1]
    notes = jnp.zeros((slot_count, LANES), F32)
    number = lax.broadcasted_iota(jnp.int32, (LANES - 2 * per, tokens), 1).astype(F32) + 1.0
    for hop, hop_pick in enumerate(picks):
        lines = jnp.concatenate([ids_ref[hop].astype(F32), codes_ref[hop], number], axis=0).astype(BF16)
        notes = notes + lax.dot_general(hop_pick, lines, ROWS_ROWS, preferred_element_type=F32)
    row_ref[:, width:] = notes.astype(BF16)


def fold(values, per):
    parts = LANES // per
    height = values.shape[0] // parts
    lane = lax.broadcasted_iota(jnp.int32, (height, LANES), 1)
    out = values[:height]
    for q in range(1, parts):
        turned = pltpu.roll(values[q * height : (q + 1) * height], q * per, 1)
        out = jnp.where(lane >= q * per, turned, out)
    return out


def score_kernel(per, row_ref, dec_ref, score_ref, ids_ref, codes_ref):
    width = dec_ref.shape[1]
    scores = lax.dot_general(row_ref[:, :width], dec_ref[...], ROWS_ROWS, preferred_element_type=F32)
    notes = row_ref[:, width:].astype(F32)
    ids = notes.astype(jnp.int32)
    low = ids & (LANES - 1)
    chosen = jnp.take_along_axis(scores[:, :LANES], low, axis=1)
    for part in range(1, dec_ref.shape[0] // LANES):
        here = jnp.take_along_axis(scores[:, part * LANES : (part + 1) * LANES], low, axis=1)
        chosen = jnp.where(ids >= part * LANES, here, chosen)
    folded = fold(chosen, per)
    for copy in range(score_ref.shape[0]):
        score_ref[copy] = folded
    ids_ref[...] = fold(notes, per).T
    codes_ref[...] = fold(pltpu.roll(notes, LANES - per, 1), per).T


def spread(ids, values, features, per):
    held = ids.shape[1]
    feature_line = lax.broadcasted_iota(jnp.int32, (features, held), 0).astype(F32)
    blocks = []
    for q in range(LANES // per):
        block = jnp.zeros((features, held), F32)
        for j in range(q * per, (q + 1) * per):
            block = jnp.where(feature_line == ids[j : j + 1, :], values[j : j + 1, :], block)
        blocks.append(block)
    return jnp.concatenate(blocks, axis=1).astype(BF16)


def back_kernel(per, score_ref, ids_ref, enc_ref, pre_ref, back_ref):
    total = score_ref[0]
    for copy in range(1, score_ref.shape[0]):
        total = total + score_ref[copy]
    rounded = total.astype(BF16).astype(F32).T
    pre = spread(ids_ref[...], rounded, enc_ref.shape[0], per)
    pre_ref[...] = pre
    back_ref[...] = lax.dot_general(pre, enc_ref[...], DEPTH_FIRST, preferred_element_type=F32).astype(BF16)


def dec_kernel(per, ids_ref, codes_ref, row_ref, out_ref):
    features, width = out_ref.shape
    code = spread(ids_ref[...], codes_ref[...], features, per)
    out_ref[...] = jnp.dot(code, row_ref[:, :width], preferred_element_type=F32).astype(BF16)


def enc_kernel(per, capacity, tokens, pre_ref, note_ref, input_ref, out_ref, turned_ref, total_ref):
    step = pl.program_id(0)

    @pl.when(step == 0)
    def _():
        turned_ref[...] = pre_ref[...].T
        total_ref[...] = jnp.zeros_like(total_ref)

    slots = note_ref.shape[0]
    number = note_ref[:, 2 * per : 2 * per + 1].astype(F32).astype(jnp.int32)
    device = lax.broadcasted_iota(jnp.int32, (slots, 1), 0) // capacity
    place = jnp.where(number > 0, device * tokens + number - 1, -1)
    line = lax.broadcasted_iota(jnp.int32, (slots, input_ref.shape[0]), 1)
    hot = (line == place).astype(F32).astype(BF16)
    here = turned_ref[pl.ds(pl.multiple_of(step * slots, slots), slots), :]
    wide = lax.dot_general(here, hot, DEPTH_FIRST, preferred_element_type=F32).astype(BF16)
    total_ref[...] += jnp.dot(wide, input_ref[...], preferred_element_type=F32)

    @pl.when(step == pl.num_programs(0) - 1)
    def _():
        out_ref[...] = total_ref[...].astype(BF16)


def merge_kernel(groups, capacity, dest_ref, back_ref, out_ref):
    picks = pick_matrices(dest_ref, groups, capacity, back_ref.shape[0])
    pick = functools.reduce(jnp.add, picks)
    out_ref[...] = lax.dot_general(pick, back_ref[...], DEPTH_FIRST, preferred_element_type=F32).astype(BF16)


def shards(enc_rows, dec_rows, inputs, out_grad, destinations, local_ids, code_values):
    groups = lax.axis_size("feat")
    slices = lax.axis_size("tok")
    tokens, hops = destinations.shape
    per = local_ids.shape[2]
    features, width = dec_rows.shape
    capacity = max(2, 2 * tokens * hops // groups)
    slots = groups * capacity
    dest = destinations.T
    shape = jax.ShapeDtypeStruct
    mac = 2 * slots * width

    every = lax.all_gather(inputs, "feat", axis=0, tiled=True)
    send_rows = call(
        functools.partial(pack_kernel, groups, capacity),
        shape((slots, width + LANES), BF16),
        mac * tokens,
        2 * slots * width + 2 * tokens * width,
    )(dest, jnp.transpose(local_ids, (1, 2, 0)), jnp.transpose(code_values, (1, 2, 0)), out_grad)
    rows = lax.all_to_all(
        send_rows.reshape(groups, capacity, width + LANES), "feat", split_axis=0, concat_axis=0, tiled=True
    ).reshape(slots, width + LANES)
    held = slots * per // LANES
    score, ids, codes = call(
        functools.partial(score_kernel, per),
        (shape((slices, held, LANES), F32), shape((LANES, held), F32), shape((LANES, held), F32)),
        mac * features,
        2 * slots * width,
    )(rows, dec_rows)
    score = lax.all_to_all(score, "tok", split_axis=0, concat_axis=0, tiled=True)
    pre, back = call(
        functools.partial(back_kernel, per),
        (shape((features, slots), BF16), shape((slots, width), BF16)),
        mac * features,
        2 * slots * width,
    )(score, ids, enc_rows)
    returned = lax.all_to_all(
        back.reshape(groups, capacity, width), "feat", split_axis=0, concat_axis=0, tiled=True
    ).reshape(slots, width)
    dec_grad = call(
        functools.partial(dec_kernel, per), shape((features, width), BF16), mac * features, 4 * slots * width
    )(ids, codes, rows)
    steps = groups // DEVICES_A_STEP
    enc_grad = call(
        functools.partial(enc_kernel, per, capacity, tokens),
        shape((features, width), BF16),
        2 * groups * tokens * features * width,
        2 * groups * tokens * width,
        grid=(steps,),
        in_specs=[
            pl.BlockSpec((features, slots), lambda i: (0, 0)),
            pl.BlockSpec((slots // steps, LANES), lambda i: (i, width // LANES)),
            pl.BlockSpec((groups * tokens // steps, width), lambda i: (i, 0)),
        ],
        out_specs=pl.BlockSpec((features, width), lambda i: (0, 0)),
        scratch_shapes=[pltpu.VMEM((slots, features), BF16), pltpu.VMEM((features, width), F32)],
    )(pre, rows, every)
    in_grad = call(
        functools.partial(merge_kernel, groups, capacity),
        shape((tokens, width), BF16),
        mac * tokens,
        4 * slots * width,
    )(dest, returned)
    return (enc_grad, dec_grad, in_grad)


def solution(mesh):
    split = P("feat", "tok")
    return jax.shard_map(
        shards,
        mesh=mesh,
        in_specs=(split, split, split, split, P("feat", None), P("feat", None, None), P("feat", None, None)),
        out_specs=(split, split, split),
        check_vma=False,
    )
```

```python
import functools

import jax
import jax.numpy as jnp
from jax import lax
from jax.experimental import pallas as pl
from jax.experimental.pallas import tpu as pltpu
from jax.sharding import PartitionSpec as P

F32 = jnp.float32
BF16 = jnp.bfloat16
LANES = 128
DEVICES_A_STEP = 4
PARTS = 4
VMEM_BYTES = 48 * 1024 * 1024
ROWS_ROWS = (((1,), (1,)), ((), ()))
DEPTH_FIRST = (((0,), (0,)), ((), ()))


def call(kernel, outs, flops, moved, operands, after=(), limit=VMEM_BYTES, **how):
    count = len(operands)

    def body(*refs):
        kernel(*refs[:count], *refs[count + len(after) :])

    specs = how.pop("in_specs", [pl.BlockSpec(memory_space=pltpu.VMEM)] * count)
    return pl.pallas_call(
        body,
        out_shape=outs,
        in_specs=list(specs) + [pl.BlockSpec(memory_space=pl.ANY)] * len(after),
        compiler_params=pltpu.CompilerParams(vmem_limit_bytes=limit),
        cost_estimate=pl.CostEstimate(flops=flops, bytes_accessed=moved, transcendentals=0),
        **how,
    )(*operands, *after)


def pick_matrices(dest_ref, groups, capacity, slot_count):
    tokens = dest_ref.shape[1]
    group_line = lax.broadcasted_iota(jnp.int32, (groups, tokens), 0)
    earlier = (
        lax.broadcasted_iota(jnp.int32, (tokens, tokens), 0)
        < lax.broadcasted_iota(jnp.int32, (tokens, tokens), 1)
    ).astype(F32).astype(BF16)
    slot_line = lax.broadcasted_iota(jnp.int32, (slot_count, tokens), 0)
    taken = jnp.zeros((groups, 1), F32)
    out = []
    for hop in range(dest_ref.shape[0]):
        dest = dest_ref[hop : hop + 1, :]
        match = (group_line == dest).astype(F32)
        before = jnp.dot(match.astype(BF16), earlier, preferred_element_type=F32) + taken
        place = jnp.sum(before * match, axis=0, keepdims=True).astype(jnp.int32)
        out.append((slot_line == dest * capacity + place).astype(F32).astype(BF16))
        taken = taken + jnp.sum(match, axis=1, keepdims=True)
    return out


def pack_kernel(groups, capacity, dest_hbm, ids_hbm, codes_hbm, grads_hbm, row_hbm, *scratch):
    dest_ref, ids_ref, codes_ref, grads_ref, row_ref, sems = scratch
    pairs = ((dest_hbm, dest_ref), (ids_hbm, ids_ref), (codes_hbm, codes_ref), (grads_hbm, grads_ref))
    copies = [pltpu.make_async_copy(a, b, sems.at[i]) for i, (a, b) in enumerate(pairs)]
    for copy in copies:
        copy.start()
    slot_count = row_ref.shape[0]
    tokens, width = grads_ref.shape
    copies[0].wait()
    picks = pick_matrices(dest_ref, groups, capacity, slot_count)
    pick = functools.reduce(jnp.add, picks)
    per = ids_ref.shape[1]
    notes = jnp.zeros((slot_count, LANES), F32)
    number = lax.broadcasted_iota(jnp.int32, (LANES - 2 * per, tokens), 1).astype(F32) + 1.0
    copies[1].wait()
    copies[2].wait()
    for hop, hop_pick in enumerate(picks):
        lines = jnp.concatenate([ids_ref[hop].astype(F32), codes_ref[hop], number], axis=0).astype(BF16)
        notes = notes + lax.dot_general(hop_pick, lines, ROWS_ROWS, preferred_element_type=F32)
    row_ref[:, width:] = notes.astype(BF16)
    copies[3].wait()
    height = slot_count // PARTS
    sends = []
    for part in range(PARTS):
        lines = slice(part * height, (part + 1) * height)
        row_ref[lines, :width] = jnp.dot(pick[lines], grads_ref[...], preferred_element_type=F32).astype(BF16)
        sends.append(pltpu.make_async_copy(row_ref.at[lines], row_hbm.at[lines], sems.at[len(copies) + part]))
        sends[-1].start()
    for send in sends:
        send.wait()


def fold(values, per):
    parts = LANES // per
    height = values.shape[0] // parts
    lane = lax.broadcasted_iota(jnp.int32, (height, LANES), 1)
    out = values[:height]
    for q in range(1, parts):
        turned = pltpu.roll(values[q * height : (q + 1) * height], q * per, 1)
        out = jnp.where(lane >= q * per, turned, out)
    return out


def score_kernel(per, row_ref, dec_ref, score_ref, ids_ref, codes_ref):
    width = dec_ref.shape[1]
    scores = lax.dot_general(row_ref[:, :width], dec_ref[...], ROWS_ROWS, preferred_element_type=F32)
    notes = row_ref[:, width:].astype(F32)
    ids = notes.astype(jnp.int32)
    low = ids & (LANES - 1)
    chosen = jnp.take_along_axis(scores[:, :LANES], low, axis=1)
    for part in range(1, dec_ref.shape[0] // LANES):
        here = jnp.take_along_axis(scores[:, part * LANES : (part + 1) * LANES], low, axis=1)
        chosen = jnp.where(ids >= part * LANES, here, chosen)
    folded = fold(chosen, per)
    for copy in range(score_ref.shape[0]):
        score_ref[copy] = folded
    ids_ref[...] = fold(notes, per).T
    codes_ref[...] = fold(pltpu.roll(notes, LANES - per, 1), per).T


def spread(ids, values, features, per):
    held = ids.shape[1]
    feature_line = lax.broadcasted_iota(jnp.int32, (features, held), 0).astype(F32)
    blocks = []
    for q in range(LANES // per):
        block = jnp.zeros((features, held), F32)
        for j in range(q * per, (q + 1) * per):
            block = jnp.where(feature_line == ids[j : j + 1, :], values[j : j + 1, :], block)
        blocks.append(block)
    return jnp.concatenate(blocks, axis=1).astype(BF16)


def back_kernel(per, score_ref, ids_ref, enc_ref, pre_ref, back_ref):
    total = score_ref[0]
    for copy in range(1, score_ref.shape[0]):
        total = total + score_ref[copy]
    rounded = total.astype(BF16).astype(F32).T
    pre = spread(ids_ref[...], rounded, enc_ref.shape[0], per)
    pre_ref[...] = pre
    back_ref[...] = lax.dot_general(pre, enc_ref[...], DEPTH_FIRST, preferred_element_type=F32).astype(BF16)


def dec_kernel(per, ids_ref, codes_ref, row_ref, out_ref):
    features, width = out_ref.shape
    code = spread(ids_ref[...], codes_ref[...], features, per)
    out_ref[...] = jnp.dot(code, row_ref[:, :width], preferred_element_type=F32).astype(BF16)


def enc_kernel(per, capacity, tokens, pre_ref, note_ref, input_ref, out_ref, turned_ref, total_ref):
    step = pl.program_id(0)

    @pl.when(step == 0)
    def _():
        turned_ref[...] = pre_ref[...].T
        total_ref[...] = jnp.zeros_like(total_ref)

    slots = note_ref.shape[0]
    number = note_ref[:, 2 * per : 2 * per + 1].astype(F32).astype(jnp.int32)
    device = lax.broadcasted_iota(jnp.int32, (slots, 1), 0) // capacity
    place = jnp.where(number > 0, device * tokens + number - 1, -1)
    line = lax.broadcasted_iota(jnp.int32, (slots, input_ref.shape[0]), 1)
    hot = (line == place).astype(F32).astype(BF16)
    here = turned_ref[pl.ds(pl.multiple_of(step * slots, slots), slots), :]
    wide = lax.dot_general(here, hot, DEPTH_FIRST, preferred_element_type=F32).astype(BF16)
    total_ref[...] += jnp.dot(wide, input_ref[...], preferred_element_type=F32)

    @pl.when(step == pl.num_programs(0) - 1)
    def _():
        out_ref[...] = total_ref[...].astype(BF16)


def merge_kernel(groups, capacity, dest_ref, back_ref, out_ref):
    picks = pick_matrices(dest_ref, groups, capacity, back_ref.shape[0])
    pick = functools.reduce(jnp.add, picks)
    out_ref[...] = lax.dot_general(pick, back_ref[...], DEPTH_FIRST, preferred_element_type=F32).astype(BF16)


def shards(enc_rows, dec_rows, inputs, out_grad, destinations, local_ids, code_values):
    groups = lax.axis_size("feat")
    slices = lax.axis_size("tok")
    tokens, hops = destinations.shape
    per = local_ids.shape[2]
    features, width = dec_rows.shape
    capacity = max(2, 2 * tokens * hops // groups)
    slots = groups * capacity
    dest = destinations.T
    shape = jax.ShapeDtypeStruct
    mac = 2 * slots * width

    every = lax.all_gather(inputs, "feat", axis=0, tiled=True)
    send_rows = call(
        functools.partial(pack_kernel, groups, capacity),
        shape((slots, width + LANES), BF16),
        mac * tokens,
        2 * slots * width + 2 * tokens * width,
        (dest, jnp.transpose(local_ids, (1, 2, 0)), jnp.transpose(code_values, (1, 2, 0)), out_grad),
        limit=None,
        in_specs=[pl.BlockSpec(memory_space=pl.ANY)] * 4,
        out_specs=pl.BlockSpec(memory_space=pl.ANY),
        scratch_shapes=[
            pltpu.VMEM((hops, tokens), jnp.int32),
            pltpu.VMEM((hops, per, tokens), jnp.int32),
            pltpu.VMEM((hops, per, tokens), F32),
            pltpu.VMEM((tokens, width), BF16),
            pltpu.VMEM((slots, width + LANES), BF16),
            pltpu.SemaphoreType.DMA((4 + PARTS,)),
        ],
    )
    rows = lax.all_to_all(
        send_rows.reshape(groups, capacity, width + LANES), "feat", split_axis=0, concat_axis=0, tiled=True
    ).reshape(slots, width + LANES)
    held = slots * per // LANES
    score, ids, codes = call(
        functools.partial(score_kernel, per),
        (shape((slices, held, LANES), F32), shape((LANES, held), F32), shape((LANES, held), F32)),
        mac * features,
        2 * slots * width,
        (rows, dec_rows),
    )
    score = lax.all_to_all(score, "tok", split_axis=0, concat_axis=0, tiled=True)
    pre, back = call(
        functools.partial(back_kernel, per),
        (shape((features, slots), BF16), shape((slots, width), BF16)),
        mac * features,
        2 * slots * width,
        (score, ids, enc_rows),
    )
    returned = lax.all_to_all(
        back.reshape(groups, capacity, width), "feat", split_axis=0, concat_axis=0, tiled=True
    ).reshape(slots, width)
    dec_grad = call(
        functools.partial(dec_kernel, per),
        shape((features, width), BF16),
        mac * features,
        4 * slots * width,
        (ids, codes, rows),
    )
    steps = groups // DEVICES_A_STEP
    enc_grad = call(
        functools.partial(enc_kernel, per, capacity, tokens),
        shape((features, width), BF16),
        2 * groups * tokens * features * width,
        2 * groups * tokens * width,
        (pre, rows, every),
        grid=(steps,),
        in_specs=[
            pl.BlockSpec((features, slots), lambda i: (0, 0)),
            pl.BlockSpec((slots // steps, LANES), lambda i: (i, width // LANES)),
            pl.BlockSpec((groups * tokens // steps, width), lambda i: (i, 0)),
        ],
        out_specs=pl.BlockSpec((features, width), lambda i: (0, 0)),
        scratch_shapes=[pltpu.VMEM((slots, features), BF16), pltpu.VMEM((features, width), F32)],
    )
    in_grad = call(
        functools.partial(merge_kernel, groups, capacity),
        shape((tokens, width), BF16),
        mac * tokens,
        4 * slots * width,
        (dest, returned),
        (enc_grad, dec_grad),
        limit=None,
    )
    return (enc_grad, dec_grad, in_grad)


def solution(mesh):
    split = P("feat", "tok")
    return jax.shard_map(
        shards,
        mesh=mesh,
        in_specs=(split, split, split, split, P("feat", None), P("feat", None, None), P("feat", None, None)),
        out_specs=(split, split, split),
        check_vma=False,
    )
```

```python
import functools

import jax
import jax.numpy as jnp
from jax import lax
from jax.experimental import pallas as pl
from jax.experimental.pallas import tpu as pltpu
from jax.sharding import PartitionSpec as P

F32 = jnp.float32
BF16 = jnp.bfloat16
LANES = 128
DEVICES_A_STEP = 4
PARTS = 4
VMEM_BYTES = 48 * 1024 * 1024
ROWS_ROWS = (((1,), (1,)), ((), ()))
DEPTH_FIRST = (((0,), (0,)), ((), ()))


def call(kernel, outs, flops, moved, operands, after=(), limit=VMEM_BYTES, **how):
    count = len(operands)

    def body(*refs):
        kernel(*refs[:count], *refs[count + len(after) :])

    specs = how.pop("in_specs", [pl.BlockSpec(memory_space=pltpu.VMEM)] * count)
    return pl.pallas_call(
        body,
        out_shape=outs,
        in_specs=list(specs) + [pl.BlockSpec(memory_space=pl.ANY)] * len(after),
        compiler_params=pltpu.CompilerParams(vmem_limit_bytes=limit),
        cost_estimate=pl.CostEstimate(flops=flops, bytes_accessed=moved, transcendentals=0),
        **how,
    )(*operands, *after)


def pick_matrices(dest_ref, groups, capacity, slot_count):
    tokens = dest_ref.shape[1]
    group_line = lax.broadcasted_iota(jnp.int32, (groups, tokens), 0)
    earlier = (
        lax.broadcasted_iota(jnp.int32, (tokens, tokens), 0)
        < lax.broadcasted_iota(jnp.int32, (tokens, tokens), 1)
    ).astype(F32).astype(BF16)
    slot_line = lax.broadcasted_iota(jnp.int32, (slot_count, tokens), 0)
    taken = jnp.zeros((groups, 1), F32)
    out = []
    for hop in range(dest_ref.shape[0]):
        dest = dest_ref[hop : hop + 1, :]
        match = (group_line == dest).astype(F32)
        before = jnp.dot(match.astype(BF16), earlier, preferred_element_type=F32) + taken
        place = jnp.sum(before * match, axis=0, keepdims=True).astype(jnp.int32)
        out.append((slot_line == dest * capacity + place).astype(F32).astype(BF16))
        taken = taken + jnp.sum(match, axis=1, keepdims=True)
    return out


def pack_kernel(groups, capacity, dest_hbm, ids_hbm, codes_hbm, grads_hbm, row_hbm, *scratch):
    dest_ref, ids_ref, codes_ref, grads_ref, row_ref, sems = scratch
    pairs = ((dest_hbm, dest_ref), (ids_hbm, ids_ref), (codes_hbm, codes_ref), (grads_hbm, grads_ref))
    copies = [pltpu.make_async_copy(a, b, sems.at[i]) for i, (a, b) in enumerate(pairs)]
    for copy in copies:
        copy.start()
    slot_count = row_ref.shape[0]
    tokens, width = grads_ref.shape
    copies[0].wait()
    picks = pick_matrices(dest_ref, groups, capacity, slot_count)
    pick = functools.reduce(jnp.add, picks)
    per = ids_ref.shape[1]
    notes = jnp.zeros((slot_count, LANES), F32)
    number = lax.broadcasted_iota(jnp.int32, (LANES - 2 * per, tokens), 1).astype(F32) + 1.0
    copies[1].wait()
    copies[2].wait()
    for hop, hop_pick in enumerate(picks):
        lines = jnp.concatenate([ids_ref[hop].astype(F32), codes_ref[hop], number], axis=0).astype(BF16)
        notes = notes + lax.dot_general(hop_pick, lines, ROWS_ROWS, preferred_element_type=F32)
    row_ref[:, width:] = notes.astype(BF16)
    copies[3].wait()
    height = slot_count // PARTS
    sends = []
    for part in range(PARTS):
        lines = slice(part * height, (part + 1) * height)
        row_ref[lines, :width] = jnp.dot(pick[lines], grads_ref[...], preferred_element_type=F32).astype(BF16)
        sends.append(pltpu.make_async_copy(row_ref.at[lines], row_hbm.at[lines], sems.at[len(copies) + part]))
        sends[-1].start()
    for send in sends:
        send.wait()


def fold(values, per):
    parts = LANES // per
    height = values.shape[0] // parts
    lane = lax.broadcasted_iota(jnp.int32, (height, LANES), 1)
    out = values[:height]
    for q in range(1, parts):
        turned = pltpu.roll(values[q * height : (q + 1) * height], q * per, 1)
        out = jnp.where(lane >= q * per, turned, out)
    return out


def score_kernel(per, row_ref, dec_ref, score_ref, ids_ref, codes_ref):
    width = dec_ref.shape[1]
    scores = lax.dot_general(row_ref[:, :width], dec_ref[...], ROWS_ROWS, preferred_element_type=F32)
    notes = row_ref[:, width:].astype(F32)
    ids = notes.astype(jnp.int32)
    low = ids & (LANES - 1)
    chosen = jnp.take_along_axis(scores[:, :LANES], low, axis=1)
    for part in range(1, dec_ref.shape[0] // LANES):
        here = jnp.take_along_axis(scores[:, part * LANES : (part + 1) * LANES], low, axis=1)
        chosen = jnp.where(ids >= part * LANES, here, chosen)
    folded = fold(chosen, per)
    for copy in range(score_ref.shape[0]):
        score_ref[copy] = folded
    ids_ref[...] = fold(notes, per).T
    codes_ref[...] = fold(pltpu.roll(notes, LANES - per, 1), per).T


def spread(ids, values, features, per):
    held = ids.shape[1]
    feature_line = lax.broadcasted_iota(jnp.int32, (features, held), 0).astype(F32)
    blocks = []
    for q in range(LANES // per):
        block = jnp.zeros((features, held), F32)
        for j in range(q * per, (q + 1) * per):
            block = jnp.where(feature_line == ids[j : j + 1, :], values[j : j + 1, :], block)
        blocks.append(block)
    return jnp.concatenate(blocks, axis=1).astype(BF16)


def back_kernel(per, score_ref, ids_ref, enc_ref, pre_ref, back_ref):
    total = score_ref[0]
    for copy in range(1, score_ref.shape[0]):
        total = total + score_ref[copy]
    rounded = total.astype(BF16).astype(F32).T
    pre = spread(ids_ref[...], rounded, enc_ref.shape[0], per)
    pre_ref[...] = pre
    back_ref[...] = lax.dot_general(pre, enc_ref[...], DEPTH_FIRST, preferred_element_type=F32).astype(BF16)


def dec_kernel(per, ids_ref, codes_ref, row_ref, out_ref):
    features, width = out_ref.shape
    code = spread(ids_ref[...], codes_ref[...], features, per)
    out_ref[...] = jnp.dot(code, row_ref[:, :width], preferred_element_type=F32).astype(BF16)


def enc_kernel(per, capacity, tokens, pre_ref, note_ref, input_ref, out_ref, mark_ref, turned_ref, total_ref):
    step = pl.program_id(0)

    @pl.when(step == 0)
    def _():
        turned_ref[...] = pre_ref[...].T
        total_ref[...] = jnp.zeros_like(total_ref)
        mark_ref[...] = jnp.zeros_like(mark_ref)

    slots = note_ref.shape[0]
    number = note_ref[:, 2 * per : 2 * per + 1].astype(F32).astype(jnp.int32)
    device = lax.broadcasted_iota(jnp.int32, (slots, 1), 0) // capacity
    place = jnp.where(number > 0, device * tokens + number - 1, -1)
    line = lax.broadcasted_iota(jnp.int32, (slots, input_ref.shape[0]), 1)
    hot = (line == place).astype(F32).astype(BF16)
    here = turned_ref[pl.ds(pl.multiple_of(step * slots, slots), slots), :]
    wide = lax.dot_general(here, hot, DEPTH_FIRST, preferred_element_type=F32).astype(BF16)
    total_ref[...] += jnp.dot(wide, input_ref[...], preferred_element_type=F32)

    @pl.when(step == pl.num_programs(0) - 1)
    def _():
        out_ref[...] = total_ref[...].astype(BF16)


def merge_kernel(groups, capacity, dest_ref, back_ref, out_ref):
    picks = pick_matrices(dest_ref, groups, capacity, back_ref.shape[0])
    pick = functools.reduce(jnp.add, picks)
    out_ref[...] = lax.dot_general(pick, back_ref[...], DEPTH_FIRST, preferred_element_type=F32).astype(BF16)


def shards(enc_rows, dec_rows, inputs, out_grad, destinations, local_ids, code_values):
    groups = lax.axis_size("feat")
    slices = lax.axis_size("tok")
    tokens, hops = destinations.shape
    per = local_ids.shape[2]
    features, width = dec_rows.shape
    capacity = max(2, 2 * tokens * hops // groups)
    slots = groups * capacity
    dest = destinations.T
    shape = jax.ShapeDtypeStruct
    mac = 2 * slots * width

    every = lax.all_gather(inputs, "feat", axis=0, tiled=True)
    send_rows = call(
        functools.partial(pack_kernel, groups, capacity),
        shape((slots, width + LANES), BF16),
        mac * tokens,
        2 * slots * width + 2 * tokens * width,
        (dest, jnp.transpose(local_ids, (1, 2, 0)), jnp.transpose(code_values, (1, 2, 0)), out_grad),
        limit=None,
        in_specs=[pl.BlockSpec(memory_space=pl.ANY)] * 4,
        out_specs=pl.BlockSpec(memory_space=pl.ANY),
        scratch_shapes=[
            pltpu.VMEM((hops, tokens), jnp.int32),
            pltpu.VMEM((hops, per, tokens), jnp.int32),
            pltpu.VMEM((hops, per, tokens), F32),
            pltpu.VMEM((tokens, width), BF16),
            pltpu.VMEM((slots, width + LANES), BF16),
            pltpu.SemaphoreType.DMA((4 + PARTS,)),
        ],
    )
    rows = lax.all_to_all(
        send_rows.reshape(groups, capacity, width + LANES), "feat", split_axis=0, concat_axis=0, tiled=True
    ).reshape(slots, width + LANES)
    held = slots * per // LANES
    score, ids, codes = call(
        functools.partial(score_kernel, per),
        (shape((slices, held, LANES), F32), shape((LANES, held), F32), shape((LANES, held), F32)),
        mac * features,
        2 * slots * width,
        (rows, dec_rows),
    )
    score = lax.all_to_all(score, "tok", split_axis=0, concat_axis=0, tiled=True)
    pre, back = call(
        functools.partial(back_kernel, per),
        (shape((features, slots), BF16), shape((slots, width), BF16)),
        mac * features,
        2 * slots * width,
        (score, ids, enc_rows),
    )
    returned = lax.all_to_all(
        back.reshape(groups, capacity, width), "feat", split_axis=0, concat_axis=0, tiled=True
    ).reshape(slots, width)
    dec_grad = call(
        functools.partial(dec_kernel, per),
        shape((features, width), BF16),
        mac * features,
        4 * slots * width,
        (ids, codes, rows),
    )
    steps = groups // DEVICES_A_STEP
    enc_grad, mark = call(
        functools.partial(enc_kernel, per, capacity, tokens),
        (shape((features, width), BF16), shape((8, LANES), F32)),
        2 * groups * tokens * features * width,
        2 * groups * tokens * width,
        (pre, rows, every),
        grid=(steps,),
        in_specs=[
            pl.BlockSpec((features, slots), lambda i: (0, 0)),
            pl.BlockSpec((slots // steps, LANES), lambda i: (i, width // LANES)),
            pl.BlockSpec((groups * tokens // steps, width), lambda i: (i, 0)),
        ],
        out_specs=(
            pl.BlockSpec((features, width), lambda i: (0, 0)),
            pl.BlockSpec((8, LANES), lambda i: (0, 0)),
        ),
        scratch_shapes=[pltpu.VMEM((slots, features), BF16), pltpu.VMEM((features, width), F32)],
    )
    in_grad = call(
        functools.partial(merge_kernel, groups, capacity),
        shape((tokens, width), BF16),
        mac * tokens,
        4 * slots * width,
        (dest, returned),
        (mark,),
    )
    return (enc_grad, dec_grad, in_grad)


def solution(mesh):
    split = P("feat", "tok")
    return jax.shard_map(
        shards,
        mesh=mesh,
        in_specs=(split, split, split, split, P("feat", None), P("feat", None, None), P("feat", None, None)),
        out_specs=(split, split, split),
        check_vma=False,
    )
```

```python
import functools

import jax
import jax.numpy as jnp
from jax import lax
from jax.experimental import pallas as pl
from jax.experimental.pallas import tpu as pltpu
from jax.sharding import PartitionSpec as P

F32 = jnp.float32
BF16 = jnp.bfloat16
LANES = 128
DEVICES_A_STEP = 4
PARTS = 4
SCALE = 128.0
VMEM_BYTES = 48 * 1024 * 1024
ROWS_ROWS = (((1,), (1,)), ((), ()))
DEPTH_FIRST = (((0,), (0,)), ((), ()))


def call(kernel, outs, flops, moved, operands, after=(), limit=VMEM_BYTES, **how):
    count = len(operands)

    def body(*refs):
        kernel(*refs[:count], *refs[count + len(after) :])

    specs = how.pop("in_specs", [pl.BlockSpec(memory_space=pltpu.VMEM)] * count)
    return pl.pallas_call(
        body,
        out_shape=outs,
        in_specs=list(specs) + [pl.BlockSpec(memory_space=pl.ANY)] * len(after),
        compiler_params=pltpu.CompilerParams(vmem_limit_bytes=limit),
        cost_estimate=pl.CostEstimate(flops=flops, bytes_accessed=moved, transcendentals=0),
        **how,
    )(*operands, *after)


def pick_matrices(dest_ref, groups, capacity, slot_count):
    tokens = dest_ref.shape[1]
    group_line = lax.broadcasted_iota(jnp.int32, (groups, tokens), 0)
    earlier = (
        lax.broadcasted_iota(jnp.int32, (tokens, tokens), 0)
        < lax.broadcasted_iota(jnp.int32, (tokens, tokens), 1)
    ).astype(F32).astype(BF16)
    slot_line = lax.broadcasted_iota(jnp.int32, (slot_count, tokens), 0)
    taken = jnp.zeros((groups, 1), F32)
    out = []
    for hop in range(dest_ref.shape[0]):
        dest = dest_ref[hop : hop + 1, :]
        match = (group_line == dest).astype(F32)
        before = jnp.dot(match.astype(BF16), earlier, preferred_element_type=F32) + taken
        place = jnp.sum(before * match, axis=0, keepdims=True).astype(jnp.int32)
        out.append((slot_line == dest * capacity + place).astype(F32).astype(BF16))
        taken = taken + jnp.sum(match, axis=1, keepdims=True)
    return out


def pack_kernel(groups, capacity, dest_hbm, ids_hbm, codes_hbm, grads_hbm, row_hbm, *scratch):
    dest_ref, ids_ref, codes_ref, grads_ref, row_ref, sems = scratch
    pairs = ((dest_hbm, dest_ref), (ids_hbm, ids_ref), (codes_hbm, codes_ref), (grads_hbm, grads_ref))
    copies = [pltpu.make_async_copy(a, b, sems.at[i]) for i, (a, b) in enumerate(pairs)]
    for copy in copies:
        copy.start()
    slot_count = row_ref.shape[0]
    tokens, width = grads_ref.shape
    copies[0].wait()
    picks = pick_matrices(dest_ref, groups, capacity, slot_count)
    pick = functools.reduce(jnp.add, picks)
    per = ids_ref.shape[1]
    notes = jnp.zeros((slot_count, LANES), F32)
    number = lax.broadcasted_iota(jnp.int32, (LANES - 2 * per, tokens), 1).astype(F32) + 1.0
    copies[1].wait()
    copies[2].wait()
    for hop, hop_pick in enumerate(picks):
        lines = jnp.concatenate([ids_ref[hop].astype(F32), codes_ref[hop], number], axis=0).astype(BF16)
        notes = notes + lax.dot_general(hop_pick, lines, ROWS_ROWS, preferred_element_type=F32)
    row_ref[:, width:] = notes.astype(BF16)
    copies[3].wait()
    height = slot_count // PARTS
    sends = []
    for part in range(PARTS):
        lines = slice(part * height, (part + 1) * height)
        row_ref[lines, :width] = jnp.dot(pick[lines], grads_ref[...], preferred_element_type=F32).astype(BF16)
        sends.append(pltpu.make_async_copy(row_ref.at[lines], row_hbm.at[lines], sems.at[len(copies) + part]))
        sends[-1].start()
    for send in sends:
        send.wait()


def fold(values, per):
    parts = LANES // per
    height = values.shape[0] // parts
    lane = lax.broadcasted_iota(jnp.int32, (height, LANES), 1)
    out = values[:height]
    for q in range(1, parts):
        turned = pltpu.roll(values[q * height : (q + 1) * height], q * per, 1)
        out = jnp.where(lane >= q * per, turned, out)
    return out


def score_kernel(per, row_ref, dec_ref, score_ref, ids_ref, codes_ref):
    width = dec_ref.shape[1]
    scores = lax.dot_general(row_ref[:, :width], dec_ref[...], ROWS_ROWS, preferred_element_type=F32)
    notes = row_ref[:, width:].astype(F32)
    ids = notes.astype(jnp.int32)
    low = ids & (LANES - 1)
    chosen = jnp.take_along_axis(scores[:, :LANES], low, axis=1)
    for part in range(1, dec_ref.shape[0] // LANES):
        here = jnp.take_along_axis(scores[:, part * LANES : (part + 1) * LANES], low, axis=1)
        chosen = jnp.where(ids >= part * LANES, here, chosen)
    score_ref[...] = fold(chosen, per)
    ids_ref[...] = fold(notes, per).T
    codes_ref[...] = fold(pltpu.roll(notes, LANES - per, 1), per).T


def spread(ids, values, features, per):
    held = ids.shape[1]
    feature_line = lax.broadcasted_iota(jnp.int32, (features, held), 0).astype(F32)
    blocks = []
    for q in range(LANES // per):
        block = jnp.zeros((features, held), F32)
        for j in range(q * per, (q + 1) * per):
            block = jnp.where(feature_line == ids[j : j + 1, :], values[j : j + 1, :], block)
        blocks.append(block)
    return jnp.concatenate(blocks, axis=1).astype(BF16)


def back_kernel(per, score_ref, ids_ref, enc_ref, pre_ref, back_ref):
    rounded = score_ref[...].astype(BF16).astype(F32).T
    pre = spread(ids_ref[...], rounded, enc_ref.shape[0], per)
    pre_ref[...] = pre
    back_ref[...] = lax.dot_general(pre, enc_ref[...], DEPTH_FIRST, preferred_element_type=F32).astype(BF16)


def dec_kernel(per, ids_ref, codes_ref, row_ref, out_ref):
    features, width = out_ref.shape
    code = spread(ids_ref[...], codes_ref[...], features, per)
    out_ref[...] = jnp.dot(code, row_ref[:, :width], preferred_element_type=F32).astype(BF16)


def enc_kernel(per, capacity, tokens, pre_ref, note_ref, input_ref, out_ref, mark_ref, turned_ref, total_ref):
    step = pl.program_id(0)

    @pl.when(step == 0)
    def _():
        turned_ref[...] = pre_ref[...].T
        total_ref[...] = jnp.zeros_like(total_ref)
        mark_ref[...] = jnp.zeros_like(mark_ref)

    slots = note_ref.shape[0]
    number = note_ref[:, 2 * per : 2 * per + 1].astype(F32).astype(jnp.int32)
    device = lax.broadcasted_iota(jnp.int32, (slots, 1), 0) // capacity
    place = jnp.where(number > 0, device * tokens + number - 1, -1)
    line = lax.broadcasted_iota(jnp.int32, (slots, input_ref.shape[0]), 1)
    hot = (line == place).astype(F32).astype(BF16)
    here = turned_ref[pl.ds(pl.multiple_of(step * slots, slots), slots), :]
    wide = lax.dot_general(here, hot, DEPTH_FIRST, preferred_element_type=F32).astype(BF16)
    total_ref[...] += jnp.dot(wide, input_ref[...], preferred_element_type=F32)

    @pl.when(step == pl.num_programs(0) - 1)
    def _():
        out_ref[...] = total_ref[...].astype(BF16)


def merge_kernel(groups, capacity, dest_ref, back_ref, out_ref):
    picks = pick_matrices(dest_ref, groups, capacity, back_ref.shape[0])
    pick = functools.reduce(jnp.add, picks)
    out_ref[...] = lax.dot_general(pick, back_ref[...], DEPTH_FIRST, preferred_element_type=F32).astype(BF16)


def shards(enc_rows, dec_rows, inputs, out_grad, destinations, local_ids, code_values):
    groups = lax.axis_size("feat")
    slices = lax.axis_size("tok")
    tokens, hops = destinations.shape
    per = local_ids.shape[2]
    features, width = dec_rows.shape
    capacity = max(2, 2 * tokens * hops // groups)
    slots = groups * capacity
    dest = destinations.T
    shape = jax.ShapeDtypeStruct
    mac = 2 * slots * width

    every = lax.all_gather(inputs, "feat", axis=0, tiled=True)
    send_rows = call(
        functools.partial(pack_kernel, groups, capacity),
        shape((slots, width + LANES), BF16),
        mac * tokens,
        2 * slots * width + 2 * tokens * width,
        (dest, jnp.transpose(local_ids, (1, 2, 0)), jnp.transpose(code_values, (1, 2, 0)), out_grad),
        limit=None,
        in_specs=[pl.BlockSpec(memory_space=pl.ANY)] * 4,
        out_specs=pl.BlockSpec(memory_space=pl.ANY),
        scratch_shapes=[
            pltpu.VMEM((hops, tokens), jnp.int32),
            pltpu.VMEM((hops, per, tokens), jnp.int32),
            pltpu.VMEM((hops, per, tokens), F32),
            pltpu.VMEM((tokens, width), BF16),
            pltpu.VMEM((slots, width + LANES), BF16),
            pltpu.SemaphoreType.DMA((4 + PARTS,)),
        ],
    )
    rows = lax.all_to_all(
        send_rows.reshape(groups, capacity, width + LANES), "feat", split_axis=0, concat_axis=0, tiled=True
    ).reshape(slots, width + LANES)
    held = slots * per // LANES
    score, ids, codes = call(
        functools.partial(score_kernel, per),
        (shape((held, LANES), F32), shape((LANES, held), F32), shape((LANES, held), F32)),
        mac * features,
        2 * slots * width,
        (rows, dec_rows),
    )
    parts = jnp.broadcast_to((score * SCALE).astype(jnp.float16), (slices, held, LANES))
    parts = lax.all_to_all(parts, "tok", split_axis=0, concat_axis=0, tiled=True)
    score = jnp.sum(parts.astype(F32), axis=0) * (1.0 / SCALE)
    pre, back = call(
        functools.partial(back_kernel, per),
        (shape((features, slots), BF16), shape((slots, width), BF16)),
        mac * features,
        2 * slots * width,
        (score, ids, enc_rows),
    )
    returned = lax.all_to_all(
        back.reshape(groups, capacity, width), "feat", split_axis=0, concat_axis=0, tiled=True
    ).reshape(slots, width)
    dec_grad = call(
        functools.partial(dec_kernel, per),
        shape((features, width), BF16),
        mac * features,
        4 * slots * width,
        (ids, codes, rows),
    )
    steps = groups // DEVICES_A_STEP
    enc_grad, mark = call(
        functools.partial(enc_kernel, per, capacity, tokens),
        (shape((features, width), BF16), shape((8, LANES), F32)),
        2 * groups * tokens * features * width,
        2 * groups * tokens * width,
        (pre, rows, every),
        grid=(steps,),
        in_specs=[
            pl.BlockSpec((features, slots), lambda i: (0, 0)),
            pl.BlockSpec((slots // steps, LANES), lambda i: (i, width // LANES)),
            pl.BlockSpec((groups * tokens // steps, width), lambda i: (i, 0)),
        ],
        out_specs=(
            pl.BlockSpec((features, width), lambda i: (0, 0)),
            pl.BlockSpec((8, LANES), lambda i: (0, 0)),
        ),
        scratch_shapes=[pltpu.VMEM((slots, features), BF16), pltpu.VMEM((features, width), F32)],
    )
    in_grad = call(
        functools.partial(merge_kernel, groups, capacity),
        shape((tokens, width), BF16),
        mac * tokens,
        4 * slots * width,
        (dest, returned),
        (mark,),
    )
    return (enc_grad, dec_grad, in_grad)


def solution(mesh):
    split = P("feat", "tok")
    return jax.shard_map(
        shards,
        mesh=mesh,
        in_specs=(split, split, split, split, P("feat", None), P("feat", None, None), P("feat", None, None)),
        out_specs=(split, split, split),
        check_vma=False,
    )
```

```python
import functools

import jax
import jax.numpy as jnp
from jax import lax
from jax.experimental import pallas as pl
from jax.experimental.pallas import tpu as pltpu
from jax.sharding import PartitionSpec as P

F32 = jnp.float32
BF16 = jnp.bfloat16
LANES = 128
DEVICES_A_STEP = 4
PARTS = 4
EARLY = 4
SCALE = 128.0
VMEM_BYTES = 48 * 1024 * 1024
ROWS_ROWS = (((1,), (1,)), ((), ()))
DEPTH_FIRST = (((0,), (0,)), ((), ()))


def call(kernel, outs, flops, moved, operands, after=(), limit=VMEM_BYTES, **how):
    count = len(operands)

    def body(*refs):
        kernel(*refs[:count], *refs[count + len(after) :])

    specs = how.pop("in_specs", [pl.BlockSpec(memory_space=pltpu.VMEM)] * count)
    return pl.pallas_call(
        body,
        out_shape=outs,
        in_specs=list(specs) + [pl.BlockSpec(memory_space=pl.ANY)] * len(after),
        compiler_params=pltpu.CompilerParams(vmem_limit_bytes=limit),
        cost_estimate=pl.CostEstimate(flops=flops, bytes_accessed=moved, transcendentals=0),
        **how,
    )(*operands, *after)


def pick_matrices(dest_ref, groups, capacity, slot_count):
    tokens = dest_ref.shape[1]
    group_line = lax.broadcasted_iota(jnp.int32, (groups, tokens), 0)
    earlier = (
        lax.broadcasted_iota(jnp.int32, (tokens, tokens), 0)
        < lax.broadcasted_iota(jnp.int32, (tokens, tokens), 1)
    ).astype(F32).astype(BF16)
    slot_line = lax.broadcasted_iota(jnp.int32, (slot_count, tokens), 0)
    taken = jnp.zeros((groups, 1), F32)
    out = []
    for hop in range(dest_ref.shape[0]):
        dest = dest_ref[hop : hop + 1, :]
        match = (group_line == dest).astype(F32)
        before = jnp.dot(match.astype(BF16), earlier, preferred_element_type=F32) + taken
        place = jnp.sum(before * match, axis=0, keepdims=True).astype(jnp.int32)
        out.append((slot_line == dest * capacity + place).astype(F32).astype(BF16))
        taken = taken + jnp.sum(match, axis=1, keepdims=True)
    return out


def pack_kernel(groups, capacity, dest_hbm, ids_hbm, codes_hbm, grads_hbm, inputs_hbm, row_hbm, early_hbm, *scratch):
    dest_ref, ids_ref, codes_ref, grads_ref, row_ref, sems = scratch
    pairs = ((dest_hbm, dest_ref), (ids_hbm, ids_ref), (codes_hbm, codes_ref), (grads_hbm, grads_ref))
    copies = [pltpu.make_async_copy(a, b, sems.at[i]) for i, (a, b) in enumerate(pairs)]
    for copy in copies:
        copy.start()
    sends = [pltpu.make_async_copy(inputs_hbm.at[: early_hbm.shape[0]], early_hbm, sems.at[len(copies)])]
    sends[0].start()
    slot_count = row_ref.shape[0]
    tokens, width = grads_ref.shape
    copies[0].wait()
    picks = pick_matrices(dest_ref, groups, capacity, slot_count)
    pick = functools.reduce(jnp.add, picks)
    per = ids_ref.shape[1]
    notes = jnp.zeros((slot_count, LANES), F32)
    number = lax.broadcasted_iota(jnp.int32, (LANES - 2 * per, tokens), 1).astype(F32) + 1.0
    copies[1].wait()
    copies[2].wait()
    for hop, hop_pick in enumerate(picks):
        lines = jnp.concatenate([ids_ref[hop].astype(F32), codes_ref[hop], number], axis=0).astype(BF16)
        notes = notes + lax.dot_general(hop_pick, lines, ROWS_ROWS, preferred_element_type=F32)
    row_ref[:, width:] = notes.astype(BF16)
    copies[3].wait()
    height = slot_count // PARTS
    for part in range(PARTS):
        lines = slice(part * height, (part + 1) * height)
        row_ref[lines, :width] = jnp.dot(pick[lines], grads_ref[...], preferred_element_type=F32).astype(BF16)
        sends.append(pltpu.make_async_copy(row_ref.at[lines], row_hbm.at[lines], sems.at[len(copies) + 1 + part]))
        sends[-1].start()
    for send in sends:
        send.wait()


def fold(values, per):
    parts = LANES // per
    height = values.shape[0] // parts
    lane = lax.broadcasted_iota(jnp.int32, (height, LANES), 1)
    out = values[:height]
    for q in range(1, parts):
        turned = pltpu.roll(values[q * height : (q + 1) * height], q * per, 1)
        out = jnp.where(lane >= q * per, turned, out)
    return out


def score_kernel(per, row_ref, dec_ref, input_ref, score_ref, ids_ref, codes_ref, late_ref):
    late_ref[...] = input_ref[input_ref.shape[0] - late_ref.shape[0] :, :]
    width = dec_ref.shape[1]
    scores = lax.dot_general(row_ref[:, :width], dec_ref[...], ROWS_ROWS, preferred_element_type=F32)
    notes = row_ref[:, width:].astype(F32)
    ids = notes.astype(jnp.int32)
    low = ids & (LANES - 1)
    chosen = jnp.take_along_axis(scores[:, :LANES], low, axis=1)
    for part in range(1, dec_ref.shape[0] // LANES):
        here = jnp.take_along_axis(scores[:, part * LANES : (part + 1) * LANES], low, axis=1)
        chosen = jnp.where(ids >= part * LANES, here, chosen)
    score_ref[...] = fold(chosen, per)
    ids_ref[...] = fold(notes, per).T
    codes_ref[...] = fold(pltpu.roll(notes, LANES - per, 1), per).T


def spread(ids, values, features, per):
    held = ids.shape[1]
    feature_line = lax.broadcasted_iota(jnp.int32, (features, held), 0).astype(F32)
    blocks = []
    for q in range(LANES // per):
        block = jnp.zeros((features, held), F32)
        for j in range(q * per, (q + 1) * per):
            block = jnp.where(feature_line == ids[j : j + 1, :], values[j : j + 1, :], block)
        blocks.append(block)
    return jnp.concatenate(blocks, axis=1).astype(BF16)


def back_kernel(per, score_ref, ids_ref, enc_ref, pre_ref, back_ref):
    rounded = score_ref[...].astype(BF16).astype(F32).T
    pre = spread(ids_ref[...], rounded, enc_ref.shape[0], per)
    pre_ref[...] = pre
    back_ref[...] = lax.dot_general(pre, enc_ref[...], DEPTH_FIRST, preferred_element_type=F32).astype(BF16)


def dec_kernel(per, ids_ref, codes_ref, row_ref, out_ref):
    features, width = out_ref.shape
    code = spread(ids_ref[...], codes_ref[...], features, per)
    out_ref[...] = jnp.dot(code, row_ref[:, :width], preferred_element_type=F32).astype(BF16)


def enc_kernel(per, capacity, tokens, pre_ref, note_ref, early_ref, late_ref, out_ref, mark_ref, turned_ref, total_ref):
    step = pl.program_id(0)

    @pl.when(step == 0)
    def _():
        turned_ref[...] = pre_ref[...].T
        total_ref[...] = jnp.zeros_like(total_ref)
        mark_ref[...] = jnp.zeros_like(mark_ref)

    slots = note_ref.shape[0]
    number = note_ref[:, 2 * per : 2 * per + 1].astype(F32).astype(jnp.int32)
    device = lax.broadcasted_iota(jnp.int32, (slots, 1), 0) // capacity
    here = turned_ref[pl.ds(pl.multiple_of(step * slots, slots), slots), :]
    first = early_ref.shape[0] * capacity // slots
    for ref, start, count in ((early_ref, 0, first), (late_ref, first, tokens - first)):
        token = number - 1 - start
        place = jnp.where((token >= 0) & (token < count), device * count + token, -1)
        line = lax.broadcasted_iota(jnp.int32, (slots, ref.shape[0]), 1)
        hot = (line == place).astype(F32).astype(BF16)
        wide = lax.dot_general(here, hot, DEPTH_FIRST, preferred_element_type=F32).astype(BF16)
        total_ref[...] += jnp.dot(wide, ref[...], preferred_element_type=F32)

    @pl.when(step == pl.num_programs(0) - 1)
    def _():
        out_ref[...] = total_ref[...].astype(BF16)


def merge_kernel(groups, capacity, dest_ref, back_ref, out_ref):
    picks = pick_matrices(dest_ref, groups, capacity, back_ref.shape[0])
    pick = functools.reduce(jnp.add, picks)
    out_ref[...] = lax.dot_general(pick, back_ref[...], DEPTH_FIRST, preferred_element_type=F32).astype(BF16)


def shards(enc_rows, dec_rows, inputs, out_grad, destinations, local_ids, code_values):
    groups = lax.axis_size("feat")
    slices = lax.axis_size("tok")
    tokens, hops = destinations.shape
    per = local_ids.shape[2]
    features, width = dec_rows.shape
    capacity = max(2, 2 * tokens * hops // groups)
    slots = groups * capacity
    dest = destinations.T
    shape = jax.ShapeDtypeStruct
    mac = 2 * slots * width

    early_count = tokens * EARLY // 8
    send_rows, early = call(
        functools.partial(pack_kernel, groups, capacity),
        (shape((slots, width + LANES), BF16), shape((early_count, width), BF16)),
        mac * tokens,
        2 * slots * width + 2 * tokens * width,
        (dest, jnp.transpose(local_ids, (1, 2, 0)), jnp.transpose(code_values, (1, 2, 0)), out_grad, inputs),
        limit=None,
        in_specs=[pl.BlockSpec(memory_space=pl.ANY)] * 5,
        out_specs=(pl.BlockSpec(memory_space=pl.ANY), pl.BlockSpec(memory_space=pl.ANY)),
        scratch_shapes=[
            pltpu.VMEM((hops, tokens), jnp.int32),
            pltpu.VMEM((hops, per, tokens), jnp.int32),
            pltpu.VMEM((hops, per, tokens), F32),
            pltpu.VMEM((tokens, width), BF16),
            pltpu.VMEM((slots, width + LANES), BF16),
            pltpu.SemaphoreType.DMA((5 + PARTS,)),
        ],
    )
    early = lax.all_gather(early, "feat", axis=0, tiled=True)
    rows = lax.all_to_all(
        send_rows.reshape(groups, capacity, width + LANES), "feat", split_axis=0, concat_axis=0, tiled=True
    ).reshape(slots, width + LANES)
    held = slots * per // LANES
    score, ids, codes, late = call(
        functools.partial(score_kernel, per),
        (
            shape((held, LANES), F32),
            shape((LANES, held), F32),
            shape((LANES, held), F32),
            shape((tokens - early_count, width), BF16),
        ),
        mac * features,
        2 * slots * width,
        (rows, dec_rows, inputs),
    )
    late = lax.all_gather(late, "feat", axis=0, tiled=True)
    parts = jnp.broadcast_to((score * SCALE).astype(jnp.float16), (slices, held, LANES))
    parts = lax.all_to_all(parts, "tok", split_axis=0, concat_axis=0, tiled=True)
    score = jnp.sum(parts.astype(F32), axis=0) * (1.0 / SCALE)
    pre, back = call(
        functools.partial(back_kernel, per),
        (shape((features, slots), BF16), shape((slots, width), BF16)),
        mac * features,
        2 * slots * width,
        (score, ids, enc_rows),
    )
    returned = lax.all_to_all(
        back.reshape(groups, capacity, width), "feat", split_axis=0, concat_axis=0, tiled=True
    ).reshape(slots, width)
    dec_grad = call(
        functools.partial(dec_kernel, per),
        shape((features, width), BF16),
        mac * features,
        4 * slots * width,
        (ids, codes, rows),
    )
    steps = groups // DEVICES_A_STEP
    enc_grad, mark = call(
        functools.partial(enc_kernel, per, capacity, tokens),
        (shape((features, width), BF16), shape((8, LANES), F32)),
        2 * groups * tokens * features * width,
        2 * groups * tokens * width,
        (pre, rows, early, late),
        grid=(steps,),
        in_specs=[
            pl.BlockSpec((features, slots), lambda i: (0, 0)),
            pl.BlockSpec((slots // steps, LANES), lambda i: (i, width // LANES)),
            pl.BlockSpec((groups * early_count // steps, width), lambda i: (i, 0)),
            pl.BlockSpec((groups * (tokens - early_count) // steps, width), lambda i: (i, 0)),
        ],
        out_specs=(
            pl.BlockSpec((features, width), lambda i: (0, 0)),
            pl.BlockSpec((8, LANES), lambda i: (0, 0)),
        ),
        scratch_shapes=[pltpu.VMEM((slots, features), BF16), pltpu.VMEM((features, width), F32)],
    )
    in_grad = call(
        functools.partial(merge_kernel, groups, capacity),
        shape((tokens, width), BF16),
        mac * tokens,
        4 * slots * width,
        (dest, returned),
        (mark,),
    )
    return (enc_grad, dec_grad, in_grad)


def solution(mesh):
    split = P("feat", "tok")
    return jax.shard_map(
        shards,
        mesh=mesh,
        in_specs=(split, split, split, split, P("feat", None), P("feat", None, None), P("feat", None, None)),
        out_specs=(split, split, split),
        check_vma=False,
    )
```

```python
import functools

import jax
import jax.numpy as jnp
from jax import lax
from jax.experimental import pallas as pl
from jax.experimental.pallas import tpu as pltpu
from jax.sharding import PartitionSpec as P

F32 = jnp.float32
BF16 = jnp.bfloat16
LANES = 128
DEVICES_A_STEP = 8
PARTS = 4
SCALE = 128.0
VMEM_BYTES = 48 * 1024 * 1024
ROWS_ROWS = (((1,), (1,)), ((), ()))
DEPTH_FIRST = (((0,), (0,)), ((), ()))


def call(kernel, outs, flops, moved, operands, after=(), limit=VMEM_BYTES, **how):
    count = len(operands)

    def body(*refs):
        kernel(*refs[:count], *refs[count + len(after) :])

    specs = how.pop("in_specs", [pl.BlockSpec(memory_space=pltpu.VMEM)] * count)
    return pl.pallas_call(
        body,
        out_shape=outs,
        in_specs=list(specs) + [pl.BlockSpec(memory_space=pl.ANY)] * len(after),
        compiler_params=pltpu.CompilerParams(vmem_limit_bytes=limit),
        cost_estimate=pl.CostEstimate(flops=flops, bytes_accessed=moved, transcendentals=0),
        **how,
    )(*operands, *after)


def places(dest_ref, groups):
    tokens = dest_ref.shape[1]
    group_line = lax.broadcasted_iota(jnp.int32, (groups, tokens), 0)
    earlier = (
        lax.broadcasted_iota(jnp.int32, (tokens, tokens), 0)
        < lax.broadcasted_iota(jnp.int32, (tokens, tokens), 1)
    ).astype(F32).astype(BF16)
    taken = jnp.zeros((groups, 1), F32)
    out = []
    for hop in range(dest_ref.shape[0]):
        match = (group_line == dest_ref[hop : hop + 1, :]).astype(F32)
        before = jnp.dot(match.astype(BF16), earlier, preferred_element_type=F32) + taken
        out.append(jnp.sum(before * match, axis=0, keepdims=True).astype(jnp.int32))
        taken = taken + jnp.sum(match, axis=1, keepdims=True)
    return out


def one_hot(numbers, count):
    line = lax.broadcasted_iota(jnp.int32, (count, numbers.shape[1]), 0)
    return (line == numbers).astype(F32).astype(BF16)


def pick_matrices(dest_ref, groups, capacity):
    return [
        one_hot(dest_ref[hop : hop + 1, :] * capacity + place, groups * capacity)
        for hop, place in enumerate(places(dest_ref, groups))
    ]


def pack_kernel(groups, capacity, dest_hbm, ids_hbm, codes_hbm, grads_hbm, inputs_hbm, message_hbm, wide_hbm, *scratch):
    dest_ref, ids_ref, codes_ref, grads_ref, message_ref, wide_ref, sems = scratch
    tokens, width = grads_ref.shape
    pairs = (
        (dest_hbm, dest_ref),
        (ids_hbm, ids_ref),
        (codes_hbm, codes_ref),
        (grads_hbm, grads_ref),
    )
    blocks = width // LANES
    pairs += tuple(
        (inputs_hbm.at[:, block * LANES : (block + 1) * LANES], wide_ref.at[block * tokens : (block + 1) * tokens, :])
        for block in range(blocks)
    )
    copies = [pltpu.make_async_copy(a, b, sems.at[i]) for i, (a, b) in enumerate(pairs)]
    for copy in copies:
        copy.start()
    per = ids_ref.shape[1]
    copies[0].wait()
    ranks = places(dest_ref, groups)
    picks = [
        one_hot(dest_ref[hop : hop + 1, :] * capacity + rank, groups * capacity) for hop, rank in enumerate(ranks)
    ]
    pick = functools.reduce(jnp.add, picks)
    info = [line.astype(F32) for hop, rank in enumerate(ranks) for line in (dest_ref[hop : hop + 1, :], rank)]
    info.append(jnp.zeros((wide_ref.shape[0] - blocks * tokens - len(info), tokens), F32))
    wide_ref[blocks * tokens :, :] = jnp.concatenate(info, axis=0).astype(BF16)
    for copy in copies[4:]:
        copy.wait()
    sends = [pltpu.make_async_copy(wide_ref, wide_hbm, sems.at[len(copies)])]
    sends[0].start()
    notes = jnp.zeros((groups * capacity, LANES), F32)
    rest = jnp.zeros((LANES - 2 * per, tokens), F32)
    copies[1].wait()
    copies[2].wait()
    for hop, hop_pick in enumerate(picks):
        lines = jnp.concatenate([ids_ref[hop].astype(F32), codes_ref[hop], rest], axis=0).astype(BF16)
        notes = notes + lax.dot_general(hop_pick, lines, ROWS_ROWS, preferred_element_type=F32)
    half = capacity // 2
    notes = notes.reshape(groups, capacity, LANES)
    low = notes[:, :half, :].reshape(groups * half, LANES)
    high = pltpu.roll(notes[:, half:, :].reshape(groups * half, LANES), 2 * per, 1)
    message_ref[:, blocks * capacity :, :] = (low + high).astype(BF16).reshape(groups, half, LANES)
    copies[3].wait()
    some = groups // PARTS
    for part in range(PARTS):
        lines = slice(part * some * capacity, (part + 1) * some * capacity)
        here = slice(part * some, (part + 1) * some)
        rows = jnp.dot(pick[lines], grads_ref[...], preferred_element_type=F32).astype(BF16)
        for block in range(blocks):
            column = rows[:, block * LANES : (block + 1) * LANES]
            message_ref[here, block * capacity : (block + 1) * capacity, :] = column.reshape(some, capacity, LANES)
        sends.append(
            pltpu.make_async_copy(message_ref.at[here], message_hbm.at[here], sems.at[len(copies) + 1 + part])
        )
        sends[-1].start()
    for send in sends:
        send.wait()


def unpack(message_ref, capacity, line_ref):
    slots = line_ref.shape[0]
    for block in range(line_ref.shape[1] // LANES):
        column = message_ref[:, block * capacity : (block + 1) * capacity, :]
        line_ref[:, block * LANES : (block + 1) * LANES] = column.reshape(slots, LANES)


def fold(values, per):
    parts = LANES // per
    height = values.shape[0] // parts
    lane = lax.broadcasted_iota(jnp.int32, (height, LANES), 1)
    out = values[:height]
    for q in range(1, parts):
        turned = pltpu.roll(values[q * height : (q + 1) * height], q * per, 1)
        out = jnp.where(lane >= q * per, turned, out)
    return out


def score_kernel(per, capacity, message_ref, dec_ref, score_ref, ids_ref, codes_ref, line_ref):
    unpack(message_ref, capacity, line_ref)
    scores = lax.dot_general(line_ref[...], dec_ref[...], ROWS_ROWS, preferred_element_type=F32)
    groups, half = message_ref.shape[0], capacity // 2
    notes = message_ref[:, message_ref.shape[1] - half :, :].astype(F32)
    turned = pltpu.roll(notes.reshape(groups * half, LANES), LANES - 2 * per, 1).reshape(groups, half, LANES)
    notes = jnp.concatenate([notes, turned], axis=1).reshape(groups * capacity, LANES)
    ids = notes.astype(jnp.int32)
    low = ids & (LANES - 1)
    chosen = jnp.take_along_axis(scores[:, :LANES], low, axis=1)
    for part in range(1, dec_ref.shape[0] // LANES):
        here = jnp.take_along_axis(scores[:, part * LANES : (part + 1) * LANES], low, axis=1)
        chosen = jnp.where(ids >= part * LANES, here, chosen)
    score_ref[...] = fold(chosen, per)
    ids_ref[...] = fold(notes, per).T
    codes_ref[...] = fold(pltpu.roll(notes, LANES - per, 1), per).T


def spread(ids, values, features, per):
    held = ids.shape[1]
    feature_line = lax.broadcasted_iota(jnp.int32, (features, held), 0).astype(F32)
    blocks = []
    for q in range(LANES // per):
        block = jnp.zeros((features, held), F32)
        for j in range(q * per, (q + 1) * per):
            block = jnp.where(feature_line == ids[j : j + 1, :], values[j : j + 1, :], block)
        blocks.append(block)
    return jnp.concatenate(blocks, axis=1).astype(BF16)


def back_kernel(per, score_ref, ids_ref, enc_ref, pre_ref, back_ref):
    rounded = score_ref[...].astype(BF16).astype(F32).T
    pre = spread(ids_ref[...], rounded, enc_ref.shape[0], per)
    pre_ref[...] = pre
    back_ref[...] = lax.dot_general(pre, enc_ref[...], DEPTH_FIRST, preferred_element_type=F32).astype(BF16)


def dec_kernel(per, capacity, ids_ref, codes_ref, message_ref, out_ref, line_ref):
    unpack(message_ref, capacity, line_ref)
    code = spread(ids_ref[...], codes_ref[...], out_ref.shape[0], per)
    out_ref[...] = jnp.dot(code, line_ref[...], preferred_element_type=F32).astype(BF16)


def enc_kernel(capacity, tokens, pre_ref, wide_ref, out_ref, mark_ref, turned_ref, total_ref, line_ref):
    step = pl.program_id(0)

    @pl.when(step == 0)
    def _():
        turned_ref[...] = pre_ref[...].T
        total_ref[...] = jnp.zeros_like(total_ref)
        mark_ref[...] = jnp.zeros_like(mark_ref)

    devices, width = wide_ref.shape[0], total_ref.shape[1]
    blocks = width // LANES
    me = lax.axis_index("feat")
    slots = []
    for device in range(devices):
        for block in range(blocks):
            line_ref[device * tokens : (device + 1) * tokens, block * LANES : (block + 1) * LANES] = wide_ref[
                device, block * tokens : (block + 1) * tokens, :
            ]
        info = wide_ref[device, blocks * tokens :, :].astype(F32).astype(jnp.int32)
        slot = jnp.where(info[2:3] == me, info[3:4] + device * capacity, -1)
        slots.append(jnp.where(info[0:1] == me, info[1:2] + device * capacity, slot))
    count = devices * capacity
    hot = one_hot(jnp.concatenate(slots, axis=1), count)
    here = turned_ref[pl.ds(pl.multiple_of(step * count, count), count), :]
    spread_out = lax.dot_general(here, hot, DEPTH_FIRST, preferred_element_type=F32).astype(BF16)
    total_ref[...] += jnp.dot(spread_out, line_ref[...], preferred_element_type=F32)

    @pl.when(step == pl.num_programs(0) - 1)
    def _():
        out_ref[...] = total_ref[...].astype(BF16)


def merge_kernel(groups, capacity, dest_ref, back_ref, out_ref):
    picks = pick_matrices(dest_ref, groups, capacity)
    pick = functools.reduce(jnp.add, picks)
    out_ref[...] = lax.dot_general(pick, back_ref[...], DEPTH_FIRST, preferred_element_type=F32).astype(BF16)


def shards(enc_rows, dec_rows, inputs, out_grad, destinations, local_ids, code_values):
    groups = lax.axis_size("feat")
    slices = lax.axis_size("tok")
    tokens, hops = destinations.shape
    per = local_ids.shape[2]
    features, width = dec_rows.shape
    capacity = max(2, 2 * tokens * hops // groups)
    slots = groups * capacity
    dest = destinations.T
    shape = jax.ShapeDtypeStruct
    mac = 2 * slots * width

    lines = capacity * width // LANES + capacity * 2 * per // LANES
    wide_lines = tokens * width // LANES + 16
    message, wide = call(
        functools.partial(pack_kernel, groups, capacity),
        (shape((groups, lines, LANES), BF16), shape((wide_lines, LANES), BF16)),
        mac * tokens,
        2 * slots * width + 4 * tokens * width,
        (dest, jnp.transpose(local_ids, (1, 2, 0)), jnp.transpose(code_values, (1, 2, 0)), out_grad, inputs),
        limit=None,
        in_specs=[pl.BlockSpec(memory_space=pl.ANY)] * 5,
        out_specs=(pl.BlockSpec(memory_space=pl.ANY), pl.BlockSpec(memory_space=pl.ANY)),
        scratch_shapes=[
            pltpu.VMEM((hops, tokens), jnp.int32),
            pltpu.VMEM((hops, per, tokens), jnp.int32),
            pltpu.VMEM((hops, per, tokens), F32),
            pltpu.VMEM((tokens, width), BF16),
            pltpu.VMEM((groups, lines, LANES), BF16),
            pltpu.VMEM((wide_lines, LANES), BF16),
            pltpu.SemaphoreType.DMA((5 + width // LANES + PARTS,)),
        ],
    )
    wide = lax.all_gather(wide, "feat", axis=0)
    message = lax.all_to_all(message, "feat", split_axis=0, concat_axis=0, tiled=True)
    held = slots * per // LANES
    score, ids, codes = call(
        functools.partial(score_kernel, per, capacity),
        (shape((held, LANES), F32), shape((LANES, held), F32), shape((LANES, held), F32)),
        mac * features,
        2 * slots * width,
        (message, dec_rows),
        scratch_shapes=[pltpu.VMEM((slots, width), BF16)],
    )
    parts = jnp.broadcast_to((score * SCALE).astype(jnp.float16), (slices, held, LANES))
    parts = lax.all_to_all(parts, "tok", split_axis=0, concat_axis=0, tiled=True)
    score = jnp.sum(parts.astype(F32), axis=0) * (1.0 / SCALE)
    pre, back = call(
        functools.partial(back_kernel, per),
        (shape((features, slots), BF16), shape((slots, width), BF16)),
        mac * features,
        2 * slots * width,
        (score, ids, enc_rows),
    )
    returned = lax.all_to_all(
        back.reshape(groups, capacity, width), "feat", split_axis=0, concat_axis=0, tiled=True
    ).reshape(slots, width)
    dec_grad = call(
        functools.partial(dec_kernel, per, capacity),
        shape((features, width), BF16),
        mac * features,
        4 * slots * width,
        (ids, codes, message),
        scratch_shapes=[pltpu.VMEM((slots, width), BF16)],
    )
    steps = groups // DEVICES_A_STEP
    enc_grad, mark = call(
        functools.partial(enc_kernel, capacity, tokens),
        (shape((features, width), BF16), shape((8, LANES), F32)),
        2 * groups * tokens * features * width,
        2 * groups * tokens * width,
        (pre, wide),
        grid=(steps,),
        in_specs=[
            pl.BlockSpec((features, slots), lambda i: (0, 0)),
            pl.BlockSpec((DEVICES_A_STEP, wide_lines, LANES), lambda i: (i, 0, 0)),
        ],
        out_specs=(
            pl.BlockSpec((features, width), lambda i: (0, 0)),
            pl.BlockSpec((8, LANES), lambda i: (0, 0)),
        ),
        scratch_shapes=[
            pltpu.VMEM((slots, features), BF16),
            pltpu.VMEM((features, width), F32),
            pltpu.VMEM((DEVICES_A_STEP * tokens, width), BF16),
        ],
    )
    in_grad = call(
        functools.partial(merge_kernel, groups, capacity),
        shape((tokens, width), BF16),
        mac * tokens,
        4 * slots * width,
        (dest, returned),
        (mark,),
    )
    return (enc_grad, dec_grad, in_grad)


def solution(mesh):
    split = P("feat", "tok")
    return jax.shard_map(
        shards,
        mesh=mesh,
        in_specs=(split, split, split, split, P("feat", None), P("feat", None, None), P("feat", None, None)),
        out_specs=(split, split, split),
        check_vma=False,
    )
```

```python
import functools

import jax
import jax.numpy as jnp
from jax import lax
from jax.experimental import pallas as pl
from jax.experimental.pallas import tpu as pltpu
from jax.sharding import PartitionSpec as P

F32 = jnp.float32
BF16 = jnp.bfloat16
LANES = 128
DEVICES_A_STEP = 8
SCALE = 128.0
VMEM_BYTES = 48 * 1024 * 1024
ROWS_ROWS = (((1,), (1,)), ((), ()))
DEPTH_FIRST = (((0,), (0,)), ((), ()))


def call(kernel, outs, flops, moved, operands, after=(), limit=VMEM_BYTES, **how):
    count = len(operands)

    def body(*refs):
        kernel(*refs[:count], *refs[count + len(after) :])

    specs = how.pop("in_specs", [pl.BlockSpec(memory_space=pltpu.VMEM)] * count)
    return pl.pallas_call(
        body,
        out_shape=outs,
        in_specs=list(specs) + [pl.BlockSpec(memory_space=pl.ANY)] * len(after),
        compiler_params=pltpu.CompilerParams(vmem_limit_bytes=limit),
        cost_estimate=pl.CostEstimate(flops=flops, bytes_accessed=moved, transcendentals=0),
        **how,
    )(*operands, *after)


def places(dest_ref, groups):
    tokens = dest_ref.shape[1]
    group_line = lax.broadcasted_iota(jnp.int32, (groups, tokens), 0)
    earlier = (
        lax.broadcasted_iota(jnp.int32, (tokens, tokens), 0)
        < lax.broadcasted_iota(jnp.int32, (tokens, tokens), 1)
    ).astype(F32).astype(BF16)
    taken = jnp.zeros((groups, 1), F32)
    out = []
    for hop in range(dest_ref.shape[0]):
        match = (group_line == dest_ref[hop : hop + 1, :]).astype(F32)
        before = jnp.dot(match.astype(BF16), earlier, preferred_element_type=F32) + taken
        out.append(jnp.sum(before * match, axis=0, keepdims=True).astype(jnp.int32))
        taken = taken + jnp.sum(match, axis=1, keepdims=True)
    return out


def one_hot(numbers, count):
    line = lax.broadcasted_iota(jnp.int32, (count, numbers.shape[1]), 0)
    return (line == numbers).astype(F32).astype(BF16)


def pick_matrices(dest_ref, groups, capacity):
    return [
        one_hot(dest_ref[hop : hop + 1, :] * capacity + place, groups * capacity)
        for hop, place in enumerate(places(dest_ref, groups))
    ]


def pack_kernel(groups, capacity, dest_hbm, ids_hbm, codes_hbm, grads_hbm, inputs_hbm, message_ref, wide_hbm, *scratch):
    dest_ref, ids_ref, codes_ref, grads_ref, wide_ref, sems = scratch
    tokens, width = grads_ref.shape
    pairs = (
        (dest_hbm, dest_ref),
        (ids_hbm, ids_ref),
        (codes_hbm, codes_ref),
        (grads_hbm, grads_ref),
    )
    blocks = width // LANES
    pairs += tuple(
        (inputs_hbm.at[:, block * LANES : (block + 1) * LANES], wide_ref.at[block * tokens : (block + 1) * tokens, :])
        for block in range(blocks)
    )
    copies = [pltpu.make_async_copy(a, b, sems.at[i]) for i, (a, b) in enumerate(pairs)]
    for copy in copies:
        copy.start()
    per = ids_ref.shape[1]
    copies[0].wait()
    ranks = places(dest_ref, groups)
    picks = [
        one_hot(dest_ref[hop : hop + 1, :] * capacity + rank, groups * capacity) for hop, rank in enumerate(ranks)
    ]
    pick = functools.reduce(jnp.add, picks)
    info = [line.astype(F32) for hop, rank in enumerate(ranks) for line in (dest_ref[hop : hop + 1, :], rank)]
    info.append(jnp.zeros((wide_ref.shape[0] - blocks * tokens - len(info), tokens), F32))
    wide_ref[blocks * tokens :, :] = jnp.concatenate(info, axis=0).astype(BF16)
    for copy in copies[4:]:
        copy.wait()
    send = pltpu.make_async_copy(wide_ref, wide_hbm, sems.at[len(copies)])
    send.start()
    notes = jnp.zeros((groups * capacity, LANES), F32)
    rest = jnp.zeros((LANES - 2 * per, tokens), F32)
    copies[1].wait()
    copies[2].wait()
    for hop, hop_pick in enumerate(picks):
        lines = jnp.concatenate([ids_ref[hop].astype(F32), codes_ref[hop], rest], axis=0).astype(BF16)
        notes = notes + lax.dot_general(hop_pick, lines, ROWS_ROWS, preferred_element_type=F32)
    half = capacity // 2
    notes = notes.reshape(groups, capacity, LANES)
    low = notes[:, :half, :].reshape(groups * half, LANES)
    high = pltpu.roll(notes[:, half:, :].reshape(groups * half, LANES), 2 * per, 1)
    message_ref[:, blocks * capacity :, :] = (low + high).astype(BF16).reshape(groups, half, LANES)
    copies[3].wait()
    rows = jnp.dot(pick, grads_ref[...], preferred_element_type=F32).astype(BF16)
    for block in range(blocks):
        column = rows[:, block * LANES : (block + 1) * LANES]
        message_ref[:, block * capacity : (block + 1) * capacity, :] = column.reshape(groups, capacity, LANES)
    send.wait()


def unpack(message_ref, capacity, line_ref):
    slots = line_ref.shape[0]
    for block in range(line_ref.shape[1] // LANES):
        column = message_ref[:, block * capacity : (block + 1) * capacity, :]
        line_ref[:, block * LANES : (block + 1) * LANES] = column.reshape(slots, LANES)


def fold(values, per):
    parts = LANES // per
    height = values.shape[0] // parts
    lane = lax.broadcasted_iota(jnp.int32, (height, LANES), 1)
    out = values[:height]
    for q in range(1, parts):
        turned = pltpu.roll(values[q * height : (q + 1) * height], q * per, 1)
        out = jnp.where(lane >= q * per, turned, out)
    return out


def score_kernel(per, capacity, message_ref, dec_ref, score_ref, ids_ref, codes_ref, line_ref):
    unpack(message_ref, capacity, line_ref)
    scores = lax.dot_general(line_ref[...], dec_ref[...], ROWS_ROWS, preferred_element_type=F32)
    groups, half = message_ref.shape[0], capacity // 2
    notes = message_ref[:, message_ref.shape[1] - half :, :].astype(F32)
    turned = pltpu.roll(notes.reshape(groups * half, LANES), LANES - 2 * per, 1).reshape(groups, half, LANES)
    notes = jnp.concatenate([notes, turned], axis=1).reshape(groups * capacity, LANES)
    ids = notes.astype(jnp.int32)
    low = ids & (LANES - 1)
    chosen = jnp.take_along_axis(scores[:, :LANES], low, axis=1)
    for part in range(1, dec_ref.shape[0] // LANES):
        here = jnp.take_along_axis(scores[:, part * LANES : (part + 1) * LANES], low, axis=1)
        chosen = jnp.where(ids >= part * LANES, here, chosen)
    score_ref[...] = fold(chosen, per)
    ids_ref[...] = fold(notes, per).T
    codes_ref[...] = fold(pltpu.roll(notes, LANES - per, 1), per).T


def spread(ids, values, features, per):
    held = ids.shape[1]
    feature_line = lax.broadcasted_iota(jnp.int32, (features, held), 0).astype(F32).astype(BF16)
    blocks = []
    for q in range(LANES // per):
        block = jnp.zeros((features, held), BF16)
        for j in range(q * per, (q + 1) * per):
            here, value = (
                jnp.concatenate([jnp.broadcast_to(a[j : j + 1, :], (16, held)).astype(BF16)] * (features // 16), axis=0)
                for a in (ids, values)
            )
            block = jnp.where(feature_line == here, value, block)
        blocks.append(block)
    return jnp.concatenate(blocks, axis=1)


def back_kernel(per, score_ref, ids_ref, enc_ref, pre_ref, back_ref):
    rounded = score_ref[...].astype(BF16).astype(F32).T
    pre = spread(ids_ref[...], rounded, enc_ref.shape[0], per)
    pre_ref[...] = pre
    back_ref[...] = lax.dot_general(pre, enc_ref[...], DEPTH_FIRST, preferred_element_type=F32).astype(BF16)


def dec_kernel(per, groups, capacity, ids_ref, codes_ref, message_ref, dest_ref, out_ref, pick_ref, line_ref):
    pick_ref[...] = functools.reduce(jnp.add, pick_matrices(dest_ref, groups, capacity)).T
    unpack(message_ref, capacity, line_ref)
    code = spread(ids_ref[...], codes_ref[...], out_ref.shape[0], per)
    out_ref[...] = jnp.dot(code, line_ref[...], preferred_element_type=F32).astype(BF16)


def enc_kernel(capacity, tokens, pre_ref, wide_ref, out_ref, mark_ref, turned_ref, total_ref, line_ref):
    step = pl.program_id(0)

    @pl.when(step == 0)
    def _():
        turned_ref[...] = pre_ref[...].T
        total_ref[...] = jnp.zeros_like(total_ref)
        mark_ref[...] = jnp.zeros_like(mark_ref)

    devices, width = wide_ref.shape[0], total_ref.shape[1]
    blocks = width // LANES
    me = lax.axis_index("feat")
    slots = []
    for device in range(devices):
        for block in range(blocks):
            line_ref[device * tokens : (device + 1) * tokens, block * LANES : (block + 1) * LANES] = wide_ref[
                device, block * tokens : (block + 1) * tokens, :
            ]
        info = wide_ref[device, blocks * tokens :, :].astype(F32).astype(jnp.int32)
        slot = jnp.where(info[2:3] == me, info[3:4] + device * capacity, -1)
        slots.append(jnp.where(info[0:1] == me, info[1:2] + device * capacity, slot))
    count = devices * capacity
    hot = one_hot(jnp.concatenate(slots, axis=1), count)
    here = turned_ref[pl.ds(pl.multiple_of(step * count, count), count), :]
    spread_out = lax.dot_general(here, hot, DEPTH_FIRST, preferred_element_type=F32).astype(BF16)
    total_ref[...] += jnp.dot(spread_out, line_ref[...], preferred_element_type=F32)

    @pl.when(step == pl.num_programs(0) - 1)
    def _():
        out_ref[...] = total_ref[...].astype(BF16)


def merge_kernel(pick_ref, back_ref, out_ref):
    out_ref[...] = jnp.dot(pick_ref[...], back_ref[...], preferred_element_type=F32).astype(BF16)


def shards(enc_rows, dec_rows, inputs, out_grad, destinations, local_ids, code_values):
    groups = lax.axis_size("feat")
    slices = lax.axis_size("tok")
    tokens, hops = destinations.shape
    per = local_ids.shape[2]
    features, width = dec_rows.shape
    capacity = max(2, 2 * tokens * hops // groups)
    slots = groups * capacity
    dest = destinations.T
    shape = jax.ShapeDtypeStruct
    mac = 2 * slots * width

    lines = capacity * width // LANES + capacity * 2 * per // LANES
    wide_lines = tokens * width // LANES + 16
    message, wide = call(
        functools.partial(pack_kernel, groups, capacity),
        (shape((groups, lines, LANES), BF16), shape((wide_lines, LANES), BF16)),
        mac * tokens,
        2 * slots * width + 4 * tokens * width,
        (dest, jnp.transpose(local_ids, (1, 2, 0)), jnp.transpose(code_values, (1, 2, 0)), out_grad, inputs),
        limit=None,
        in_specs=[pl.BlockSpec(memory_space=pl.ANY)] * 5,
        out_specs=(pl.BlockSpec(memory_space=pltpu.VMEM), pl.BlockSpec(memory_space=pl.ANY)),
        scratch_shapes=[
            pltpu.VMEM((hops, tokens), jnp.int32),
            pltpu.VMEM((hops, per, tokens), jnp.int32),
            pltpu.VMEM((hops, per, tokens), F32),
            pltpu.VMEM((tokens, width), BF16),
            pltpu.VMEM((wide_lines, LANES), BF16),
            pltpu.SemaphoreType.DMA((5 + width // LANES,)),
        ],
    )
    wide = lax.all_gather(wide, "feat", axis=0)
    message = lax.all_to_all(message, "feat", split_axis=0, concat_axis=0, tiled=True)
    held = slots * per // LANES
    score, ids, codes = call(
        functools.partial(score_kernel, per, capacity),
        (shape((held, LANES), F32), shape((LANES, held), F32), shape((LANES, held), F32)),
        mac * features,
        2 * slots * width,
        (message, dec_rows),
        scratch_shapes=[pltpu.VMEM((slots, width), BF16)],
    )
    parts = jnp.broadcast_to((score * SCALE).astype(jnp.float16), (slices, held, LANES))
    parts = lax.all_to_all(parts, "tok", split_axis=0, concat_axis=0, tiled=True)
    score = jnp.sum(parts.astype(F32), axis=0) * (1.0 / SCALE)
    pre, back = call(
        functools.partial(back_kernel, per),
        (shape((features, slots), BF16), shape((slots, width), BF16)),
        mac * features,
        2 * slots * width,
        (score, ids, enc_rows),
    )
    returned = lax.all_to_all(
        back.reshape(groups, capacity, width), "feat", split_axis=0, concat_axis=0, tiled=True
    ).reshape(slots, width)
    dec_grad, pick = call(
        functools.partial(dec_kernel, per, groups, capacity),
        (shape((features, width), BF16), shape((tokens, slots), BF16)),
        mac * features,
        4 * slots * width,
        (ids, codes, message, dest),
        scratch_shapes=[pltpu.VMEM((slots, width), BF16)],
    )
    steps = groups // DEVICES_A_STEP
    enc_grad, mark = call(
        functools.partial(enc_kernel, capacity, tokens),
        (shape((features, width), BF16), shape((8, LANES), F32)),
        2 * groups * tokens * features * width,
        2 * groups * tokens * width,
        (pre, wide),
        grid=(steps,),
        in_specs=[
            pl.BlockSpec((features, slots), lambda i: (0, 0)),
            pl.BlockSpec((DEVICES_A_STEP, wide_lines, LANES), lambda i: (i, 0, 0)),
        ],
        out_specs=(
            pl.BlockSpec((features, width), lambda i: (0, 0)),
            pl.BlockSpec((8, LANES), lambda i: (0, 0)),
        ),
        scratch_shapes=[
            pltpu.VMEM((slots, features), BF16),
            pltpu.VMEM((features, width), F32),
            pltpu.VMEM((DEVICES_A_STEP * tokens, width), BF16),
        ],
    )
    in_grad = call(
        merge_kernel,
        shape((tokens, width), BF16),
        mac * tokens,
        4 * slots * width,
        (pick, returned),
        (mark,),
    )
    return (enc_grad, dec_grad, in_grad)


def solution(mesh):
    split = P("feat", "tok")
    return jax.shard_map(
        shards,
        mesh=mesh,
        in_specs=(split, split, split, split, P("feat", None), P("feat", None, None), P("feat", None, None)),
        out_specs=(split, split, split),
        check_vma=False,
    )
```

```python
import functools

import jax
import jax.numpy as jnp
from jax import lax
from jax.experimental import pallas as pl
from jax.experimental.pallas import tpu as pltpu
from jax.sharding import PartitionSpec as P

F32 = jnp.float32
BF16 = jnp.bfloat16
LANES = 128
DEVICES_A_STEP = 8
SCALE = 128.0
VMEM_BYTES = 48 * 1024 * 1024
ROWS_ROWS = (((1,), (1,)), ((), ()))
DEPTH_FIRST = (((0,), (0,)), ((), ()))


def call(kernel, outs, flops, moved, operands, after=(), limit=VMEM_BYTES, **how):
    count = len(operands)

    def body(*refs):
        kernel(*refs[:count], *refs[count + len(after) :])

    specs = how.pop("in_specs", [pl.BlockSpec(memory_space=pltpu.VMEM)] * count)
    return pl.pallas_call(
        body,
        out_shape=outs,
        in_specs=list(specs) + [pl.BlockSpec(memory_space=pl.ANY)] * len(after),
        compiler_params=pltpu.CompilerParams(vmem_limit_bytes=limit),
        cost_estimate=pl.CostEstimate(flops=flops, bytes_accessed=moved, transcendentals=0),
        **how,
    )(*operands, *after)


def places(dest_ref, groups):
    tokens = dest_ref.shape[1]
    group_line = lax.broadcasted_iota(jnp.int32, (groups, tokens), 0)
    earlier = (
        lax.broadcasted_iota(jnp.int32, (tokens, tokens), 0)
        < lax.broadcasted_iota(jnp.int32, (tokens, tokens), 1)
    ).astype(F32).astype(BF16)
    taken = jnp.zeros((groups, 1), F32)
    out = []
    for hop in range(dest_ref.shape[0]):
        match = (group_line == dest_ref[hop : hop + 1, :]).astype(F32)
        before = jnp.dot(match.astype(BF16), earlier, preferred_element_type=F32) + taken
        out.append(jnp.sum(before * match, axis=0, keepdims=True).astype(jnp.int32))
        taken = taken + jnp.sum(match, axis=1, keepdims=True)
    return out


def one_hot(numbers, count):
    line = lax.broadcasted_iota(jnp.int32, (count, numbers.shape[1]), 0)
    return (line == numbers).astype(F32).astype(BF16)


def pick_matrices(dest_ref, groups, capacity):
    return [
        one_hot(dest_ref[hop : hop + 1, :] * capacity + place, groups * capacity)
        for hop, place in enumerate(places(dest_ref, groups))
    ]


def pack_kernel(groups, capacity, dest_hbm, ids_hbm, codes_hbm, grads_hbm, inputs_hbm, message_ref, wide_hbm, *scratch):
    dest_ref, ids_ref, codes_ref, grads_ref, wide_ref, sems = scratch
    tokens, width = grads_ref.shape
    pairs = (
        (dest_hbm, dest_ref),
        (ids_hbm, ids_ref),
        (codes_hbm, codes_ref),
        (grads_hbm, grads_ref),
    )
    blocks = width // LANES
    pairs += tuple(
        (inputs_hbm.at[:, block * LANES : (block + 1) * LANES], wide_ref.at[block * tokens : (block + 1) * tokens, :])
        for block in range(blocks)
    )
    copies = [pltpu.make_async_copy(a, b, sems.at[i]) for i, (a, b) in enumerate(pairs)]
    for copy in copies:
        copy.start()
    per = ids_ref.shape[1]
    copies[0].wait()
    ranks = places(dest_ref, groups)
    picks = [
        one_hot(dest_ref[hop : hop + 1, :] * capacity + rank, groups * capacity) for hop, rank in enumerate(ranks)
    ]
    pick = functools.reduce(jnp.add, picks)
    info = [line.astype(F32) for hop, rank in enumerate(ranks) for line in (dest_ref[hop : hop + 1, :], rank)]
    info.append(jnp.zeros((wide_ref.shape[0] - blocks * tokens - len(info), tokens), F32))
    wide_ref[blocks * tokens :, :] = jnp.concatenate(info, axis=0).astype(BF16)
    for copy in copies[4:]:
        copy.wait()
    send = pltpu.make_async_copy(wide_ref, wide_hbm, sems.at[len(copies)])
    send.start()
    notes = jnp.zeros((groups * capacity, LANES), F32)
    rest = jnp.zeros((LANES - 2 * per, tokens), F32)
    copies[1].wait()
    copies[2].wait()
    for hop, hop_pick in enumerate(picks):
        lines = jnp.concatenate([ids_ref[hop].astype(F32), codes_ref[hop], rest], axis=0).astype(BF16)
        notes = notes + lax.dot_general(hop_pick, lines, ROWS_ROWS, preferred_element_type=F32)
    half = capacity // 2
    notes = notes.reshape(groups, capacity, LANES)
    low = notes[:, :half, :].reshape(groups * half, LANES)
    high = pltpu.roll(notes[:, half:, :].reshape(groups * half, LANES), 2 * per, 1)
    message_ref[:, blocks * capacity :, :] = (low + high).astype(BF16).reshape(groups, half, LANES)
    copies[3].wait()
    rows = jnp.dot(pick, grads_ref[...], preferred_element_type=F32).astype(BF16)
    for block in range(blocks):
        column = rows[:, block * LANES : (block + 1) * LANES]
        message_ref[:, block * capacity : (block + 1) * capacity, :] = column.reshape(groups, capacity, LANES)
    send.wait()


def unpack(message_ref, capacity, line_ref):
    slots = line_ref.shape[0]
    for block in range(line_ref.shape[1] // LANES):
        column = message_ref[:, block * capacity : (block + 1) * capacity, :]
        line_ref[:, block * LANES : (block + 1) * LANES] = column.reshape(slots, LANES)


def fold(values, per):
    parts = LANES // per
    height = values.shape[0] // parts
    lane = lax.broadcasted_iota(jnp.int32, (height, LANES), 1)
    out = values[:height]
    for q in range(1, parts):
        turned = pltpu.roll(values[q * height : (q + 1) * height], q * per, 1)
        out = jnp.where(lane >= q * per, turned, out)
    return out


def score_kernel(per, capacity, message_ref, dec_ref, score_ref, ids_ref, codes_ref, line_ref):
    unpack(message_ref, capacity, line_ref)
    scores = lax.dot_general(line_ref[...], dec_ref[...], ROWS_ROWS, preferred_element_type=F32)
    groups, half = message_ref.shape[0], capacity // 2
    notes = message_ref[:, message_ref.shape[1] - half :, :].astype(F32)
    turned = pltpu.roll(notes.reshape(groups * half, LANES), LANES - 2 * per, 1).reshape(groups, half, LANES)
    notes = jnp.concatenate([notes, turned], axis=1).reshape(groups * capacity, LANES)
    ids = notes.astype(jnp.int32)
    low = ids & (LANES - 1)
    chosen = jnp.take_along_axis(scores[:, :LANES], low, axis=1)
    for part in range(1, dec_ref.shape[0] // LANES):
        here = jnp.take_along_axis(scores[:, part * LANES : (part + 1) * LANES], low, axis=1)
        chosen = jnp.where(ids >= part * LANES, here, chosen)
    score_ref[...] = fold(chosen, per)
    ids_ref[...] = fold(notes, per).T
    codes_ref[...] = fold(pltpu.roll(notes, LANES - per, 1), per).T


def spread(ids, values, features, per):
    held = ids.shape[1]
    feature_line = lax.broadcasted_iota(jnp.int32, (features, held), 0).astype(F32).astype(BF16)
    blocks = []
    for q in range(LANES // per):
        block = jnp.zeros((features, held), BF16)
        for j in range(q * per, (q + 1) * per):
            here, value = (
                jnp.concatenate([jnp.broadcast_to(a[j : j + 1, :], (16, held)).astype(BF16)] * (features // 16), axis=0)
                for a in (ids, values)
            )
            block = jnp.where(feature_line == here, value, block)
        blocks.append(block)
    return jnp.concatenate(blocks, axis=1)


def inverse_kernel(per, ids_ref, inverse_ref):
    count, held = ids_ref.shape
    lane = lax.broadcasted_iota(jnp.int32, (count, held), 0).astype(F32) + 1.0
    inverse_ref[...] = spread(ids_ref[...], lane, inverse_ref.shape[1], per).astype(F32).T.astype(jnp.int32) - 1


def back_kernel(score_ref, inverse_ref, enc_ref, pre_ref, back_ref):
    held = score_ref.shape[0]
    rounded = score_ref[...].astype(BF16).astype(F32)
    slots, features = inverse_ref.shape
    for q in range(slots // held):
        for part in range(features // LANES):
            lane = inverse_ref[q * held : (q + 1) * held, part * LANES : (part + 1) * LANES]
            value = jnp.take_along_axis(rounded, jnp.maximum(lane, 0), axis=1)
            pre_ref[q * held : (q + 1) * held, part * LANES : (part + 1) * LANES] = jnp.where(
                lane >= 0, value, 0.0
            ).astype(BF16)
    back_ref[...] = jnp.dot(pre_ref[...], enc_ref[...], preferred_element_type=F32).astype(BF16)


def dec_kernel(per, groups, capacity, ids_ref, codes_ref, message_ref, dest_ref, out_ref, pick_ref, line_ref):
    pick_ref[...] = functools.reduce(jnp.add, pick_matrices(dest_ref, groups, capacity)).T
    unpack(message_ref, capacity, line_ref)
    code = spread(ids_ref[...], codes_ref[...], out_ref.shape[0], per)
    out_ref[...] = jnp.dot(code, line_ref[...], preferred_element_type=F32).astype(BF16)


def enc_kernel(capacity, tokens, pre_ref, wide_ref, out_ref, mark_ref, total_ref, line_ref):
    step = pl.program_id(0)

    @pl.when(step == 0)
    def _():
        total_ref[...] = jnp.zeros_like(total_ref)
        mark_ref[...] = jnp.zeros_like(mark_ref)

    devices, width = wide_ref.shape[0], total_ref.shape[1]
    blocks = width // LANES
    me = lax.axis_index("feat")
    slots = []
    for device in range(devices):
        for block in range(blocks):
            line_ref[device * tokens : (device + 1) * tokens, block * LANES : (block + 1) * LANES] = wide_ref[
                device, block * tokens : (block + 1) * tokens, :
            ]
        info = wide_ref[device, blocks * tokens :, :].astype(F32).astype(jnp.int32)
        slot = jnp.where(info[2:3] == me, info[3:4] + device * capacity, -1)
        slots.append(jnp.where(info[0:1] == me, info[1:2] + device * capacity, slot))
    count = devices * capacity
    hot = one_hot(jnp.concatenate(slots, axis=1), count)
    spread_out = lax.dot_general(pre_ref[...], hot, DEPTH_FIRST, preferred_element_type=F32).astype(BF16)
    total_ref[...] += jnp.dot(spread_out, line_ref[...], preferred_element_type=F32)

    @pl.when(step == pl.num_programs(0) - 1)
    def _():
        out_ref[...] = total_ref[...].astype(BF16)


def merge_kernel(pick_ref, back_ref, out_ref):
    out_ref[...] = jnp.dot(pick_ref[...], back_ref[...], preferred_element_type=F32).astype(BF16)


def shards(enc_rows, dec_rows, inputs, out_grad, destinations, local_ids, code_values):
    groups = lax.axis_size("feat")
    slices = lax.axis_size("tok")
    tokens, hops = destinations.shape
    per = local_ids.shape[2]
    features, width = dec_rows.shape
    capacity = max(2, 2 * tokens * hops // groups)
    slots = groups * capacity
    dest = destinations.T
    shape = jax.ShapeDtypeStruct
    mac = 2 * slots * width

    lines = capacity * width // LANES + capacity * 2 * per // LANES
    wide_lines = tokens * width // LANES + 16
    message, wide = call(
        functools.partial(pack_kernel, groups, capacity),
        (shape((groups, lines, LANES), BF16), shape((wide_lines, LANES), BF16)),
        mac * tokens,
        2 * slots * width + 4 * tokens * width,
        (dest, jnp.transpose(local_ids, (1, 2, 0)), jnp.transpose(code_values, (1, 2, 0)), out_grad, inputs),
        limit=None,
        in_specs=[pl.BlockSpec(memory_space=pl.ANY)] * 5,
        out_specs=(pl.BlockSpec(memory_space=pltpu.VMEM), pl.BlockSpec(memory_space=pl.ANY)),
        scratch_shapes=[
            pltpu.VMEM((hops, tokens), jnp.int32),
            pltpu.VMEM((hops, per, tokens), jnp.int32),
            pltpu.VMEM((hops, per, tokens), F32),
            pltpu.VMEM((tokens, width), BF16),
            pltpu.VMEM((wide_lines, LANES), BF16),
            pltpu.SemaphoreType.DMA((5 + width // LANES,)),
        ],
    )
    wide = lax.all_gather(wide, "feat", axis=0)
    message = lax.all_to_all(message, "feat", split_axis=0, concat_axis=0, tiled=True)
    held = slots * per // LANES
    score, ids, codes = call(
        functools.partial(score_kernel, per, capacity),
        (shape((held, LANES), F32), shape((LANES, held), F32), shape((LANES, held), F32)),
        mac * features,
        2 * slots * width,
        (message, dec_rows),
        scratch_shapes=[pltpu.VMEM((slots, width), BF16)],
    )
    parts = jnp.broadcast_to((score * SCALE).astype(jnp.float16), (slices, held, LANES))
    parts = lax.all_to_all(parts, "tok", split_axis=0, concat_axis=0, tiled=True)
    score = jnp.sum(parts.astype(F32), axis=0) * (1.0 / SCALE)
    inverse = call(
        functools.partial(inverse_kernel, per),
        shape((slots, features), jnp.int32),
        2 * slots * features * per,
        4 * slots * features,
        (ids,),
    )
    pre, back = call(
        back_kernel,
        (shape((slots, features), BF16), shape((slots, width), BF16)),
        mac * features,
        2 * slots * width,
        (score, inverse, enc_rows),
    )
    returned = lax.all_to_all(
        back.reshape(groups, capacity, width), "feat", split_axis=0, concat_axis=0, tiled=True
    ).reshape(slots, width)
    dec_grad, pick = call(
        functools.partial(dec_kernel, per, groups, capacity),
        (shape((features, width), BF16), shape((tokens, slots), BF16)),
        mac * features,
        4 * slots * width,
        (ids, codes, message, dest),
        scratch_shapes=[pltpu.VMEM((slots, width), BF16)],
    )
    steps = groups // DEVICES_A_STEP
    enc_grad, mark = call(
        functools.partial(enc_kernel, capacity, tokens),
        (shape((features, width), BF16), shape((8, LANES), F32)),
        2 * groups * tokens * features * width,
        2 * groups * tokens * width,
        (pre, wide),
        grid=(steps,),
        in_specs=[
            pl.BlockSpec((slots // steps, features), lambda i: (i, 0)),
            pl.BlockSpec((DEVICES_A_STEP, wide_lines, LANES), lambda i: (i, 0, 0)),
        ],
        out_specs=(
            pl.BlockSpec((features, width), lambda i: (0, 0)),
            pl.BlockSpec((8, LANES), lambda i: (0, 0)),
        ),
        scratch_shapes=[
            pltpu.VMEM((features, width), F32),
            pltpu.VMEM((DEVICES_A_STEP * tokens, width), BF16),
        ],
    )
    in_grad = call(
        merge_kernel,
        shape((tokens, width), BF16),
        mac * tokens,
        4 * slots * width,
        (pick, returned),
        (mark,),
    )
    return (enc_grad, dec_grad, in_grad)


def solution(mesh):
    split = P("feat", "tok")
    return jax.shard_map(
        shards,
        mesh=mesh,
        in_specs=(split, split, split, split, P("feat", None), P("feat", None, None), P("feat", None, None)),
        out_specs=(split, split, split),
        check_vma=False,
    )
```
